256 devices in a mesh: dp: 8 (over x, core), expert: 32 (over y, z).
Axes of the slice: x: 4, y: 4, z: 8, core: 2. Of those that a mesh axis runs over, the one named last changes fastest.
Arguments:
- tokens: bfloat16 [8192, 4096], P('expert', 'dp'), may hold values from -6 to 6
- out_grad: bfloat16 [8192, 4096], P('expert', 'dp'), may hold values from -1.5 to 1.5
- slot_token: int32 [32, 64, 16], P('expert'), may hold values from -1 to 255, as said below
- slot_gate: bfloat16 [32, 64, 16], P('expert'), may hold values from 0.099609375 to 1
- w_gate: bfloat16 [64, 4096, 768], P('expert', 'dp'), may hold values from -0.09375 to 0.09375
- w_up: bfloat16 [64, 4096, 768], P('expert', 'dp'), may hold values from -0.09375 to 0.09375
- w_down: bfloat16 [64, 768, 4096], P('expert', None, 'dp'), may hold values from -0.21875 to 0.21875
Outputs:
- moe_out: bfloat16 [8192, 4096], P('expert', 'dp')
- token_grad: bfloat16 [8192, 4096], P('expert', 'dp')
- gate_grad: bfloat16 [32, 64, 16], P('expert')
- grad_w_gate: bfloat16 [64, 4096, 768], P('expert', 'dp')
- grad_w_up: bfloat16 [64, 4096, 768], P('expert', 'dp')
- grad_w_down: bfloat16 [64, 768, 4096], P('expert', None, 'dp')
The draws below stay inside these ranges and needn't reach their ends.
Inputs may be any that keep to these rules, and one draw needn't show every extreme that they name: `slot_token`: entry [s, e, j] is the row, among sender s's 256 tokens, that slot j of expert e takes from s, or -1 for an empty slot; the rows of one sender and expert are distinct; every expert has exactly 256 non-empty slots in all, at most 16 from one sender, and for every expert some sender fills all 16.
All inputs are finite; a program needn't handle non-finite values.
Results may differ from the reference program's by a relative error of at most 0.0064.
Values may be sent and summed in bfloat16 or wider, within the bound.
No kernel may reach another device: no remote copies, remote signals or barrier semaphores. Data moves between devices by JAX's collectives and lax.ppermute only.
A program may use at most 128 MiB of HBM per device.

```python
import math
import jax
import jax.numpy as jnp
from jax import lax

D = 4096
FF = 768
TOK_DEV = 256
EXPERTS = 64
TOKENS = 8192
PAIR = 16
ROWS = 512
N_EXPERT = 32


def draw_slot_token(key, part):
    key = jax.random.fold_in(key, 11)
    fill_key, order_key, pick_key, place_key = jax.random.split(key, 4)
    half_count = N_EXPERT // 2
    sender_order = jax.vmap(lambda one_key: jax.random.permutation(one_key, N_EXPERT))(jax.random.split(order_key, EXPERTS))
    first_load = jax.random.randint(fill_key, (EXPERTS, half_count), 0, PAIR + 1)
    first_load = first_load.at[:, 0].set(PAIR)
    paired_load = jnp.concatenate([first_load, PAIR - first_load], axis=1).astype(jnp.int32)
    expert_rows = jnp.arange(EXPERTS, dtype=jnp.int32)[:, None]
    loads = jnp.zeros((EXPERTS, N_EXPERT), jnp.int32).at[expert_rows, sender_order].set(paired_load)
    loads = jnp.transpose(loads).reshape(N_EXPERT * EXPERTS)
    picks = jax.vmap(lambda one_key: jax.random.permutation(one_key, TOK_DEV)[:PAIR])(jax.random.split(pick_key, N_EXPERT * EXPERTS))
    ranks = jax.vmap(lambda one_key: jax.random.permutation(one_key, PAIR))(jax.random.split(place_key, N_EXPERT * EXPERTS))
    chosen = jnp.take_along_axis(picks, ranks, axis=1)
    filled = jnp.where(ranks < loads[:, None], chosen, -1).astype(jnp.int32)
    return filled.reshape(N_EXPERT, EXPERTS, PAIR)


def level_of(rng, extent, pieces, low, largest):
    def one(dim, shards_of):
        draws = jax.random.uniform(jax.random.fold_in(jax.random.fold_in(rng, 6), dim), (shards_of,), jnp.float32, low / len(pieces), largest / len(pieces))
        return jnp.repeat(jnp.exp(draws), extent[dim] // shards_of).reshape((-1,) + (1,) * (len(extent) - dim - 1))

    level = one(*pieces[0])
    for cut in pieces[1:]:
        level = level * one(*cut)
    return level


def normal_values(stream_key, dims, scale, most, cuts=(), kind=jnp.bfloat16):
    values = jax.random.normal(stream_key, dims, jnp.float32) * scale
    if len(cuts) > 0:
        values = level_of(stream_key, dims, cuts, -0.22, 0.18) * values
    return jnp.clip(values, min=-most, max=most).astype(kind)


def setup_inputs(seed: int = 0) -> dict:
    keys = jax.random.split(jax.random.key(seed), 8)
    tokens = normal_values(keys[0], (TOKENS, D), 1.0, 6.0, ((0, 32), (1, 8)))
    out_grad = normal_values(keys[1], (TOKENS, D), 0.25, 1.5, ((0, 32), (1, 8)))
    slot_token = draw_slot_token(jax.random.fold_in(keys[7], 71), 0)
    slot_gate = jnp.clip(jnp.exp(math.log(1.0) - 2.306499 * jax.random.uniform(keys[3], (N_EXPERT, EXPERTS, PAIR), jnp.float32) ** level_of(keys[3], (N_EXPERT, EXPERTS, PAIR), ((0, 32),), -0.2, 0.2)), 0.099609375, 1.0).astype(jnp.bfloat16)
    w_gate = normal_values(keys[4], (EXPERTS, D, FF), D ** -0.5, 0.09375, ((0, 32), (1, 8)))
    w_up = normal_values(keys[5], (EXPERTS, D, FF), D ** -0.5, 0.09375, ((0, 32), (1, 8)))
    w_down = normal_values(keys[6], (EXPERTS, FF, D), FF ** -0.5, 0.21875, ((0, 32), (2, 8)))
    return {"tokens": tokens, "out_grad": out_grad, "slot_token": slot_token, "slot_gate": slot_gate, "w_gate": w_gate, "w_up": w_up, "w_down": w_down}


def silu_slope(values):
    sigma = jax.nn.sigmoid(values)
    return sigma * (1.0 + values * (1.0 - sigma))


def expert_pass(tokens, out_grad, packed):
    token_ids, live_slots, gate_values, w_gate, w_up, w_down = packed
    rows_in = jnp.where(live_slots[:, None], tokens[token_ids], jnp.zeros((), jnp.bfloat16))
    rows_grad = jnp.where(live_slots[:, None], out_grad[token_ids], jnp.zeros((), jnp.bfloat16))
    gate_pre = jnp.dot(rows_in, w_gate, preferred_element_type=jnp.float32)
    up_pre = jnp.dot(rows_in, w_up, preferred_element_type=jnp.float32)
    activated = jax.nn.silu(gate_pre)
    hidden = (activated * up_pre).astype(jnp.bfloat16)
    expert_out = jnp.dot(hidden, w_down, preferred_element_type=jnp.float32)
    weighted = (gate_values[:, None] * expert_out).astype(jnp.bfloat16)
    grad_float = rows_grad.astype(jnp.float32)
    gate_dots = jnp.sum(expert_out * grad_float, axis=1).astype(jnp.bfloat16)
    scaled_grad = (gate_values[:, None] * grad_float).astype(jnp.bfloat16)
    hidden_grad = jnp.dot(scaled_grad, w_down.T, preferred_element_type=jnp.float32)
    gate_pre_grad = (hidden_grad * up_pre * silu_slope(gate_pre)).astype(jnp.bfloat16)
    up_pre_grad = (hidden_grad * activated).astype(jnp.bfloat16)
    rows_back = (jnp.dot(gate_pre_grad, w_gate.T, preferred_element_type=jnp.float32)
                 + jnp.dot(up_pre_grad, w_up.T, preferred_element_type=jnp.float32)).astype(jnp.bfloat16)
    grad_gate_w = jnp.dot(rows_in.T, gate_pre_grad, preferred_element_type=jnp.float32).astype(jnp.bfloat16)
    grad_up_w = jnp.dot(rows_in.T, up_pre_grad, preferred_element_type=jnp.float32).astype(jnp.bfloat16)
    grad_down_w = jnp.dot(hidden.T, scaled_grad, preferred_element_type=jnp.float32).astype(jnp.bfloat16)
    return weighted, rows_back, gate_dots, grad_gate_w, grad_up_w, grad_down_w


def reference(tokens, out_grad, slot_token, slot_gate, w_gate, w_up, w_down):
    sender_base = (jnp.arange(N_EXPERT, dtype=jnp.int32) * TOK_DEV)[:, None, None]
    live_mask = slot_token >= 0
    global_ids = jnp.where(live_mask, slot_token + sender_base, 0).astype(jnp.int32)
    token_ids = jnp.transpose(global_ids, (1, 0, 2)).reshape(EXPERTS, ROWS)
    live_slots = jnp.transpose(live_mask, (1, 0, 2)).reshape(EXPERTS, ROWS)
    gate_values = jnp.transpose(slot_gate, (1, 0, 2)).reshape(EXPERTS, ROWS).astype(jnp.float32)
    outputs = lax.map(lambda packed: expert_pass(tokens, out_grad, packed),
                      (token_ids, live_slots, gate_values, w_gate, w_up, w_down))
    weighted, rows_back, gate_dots, grad_gate_w, grad_up_w, grad_down_w = outputs
    flat_ids = token_ids.reshape(EXPERTS * ROWS)
    moe_out = jnp.zeros((TOKENS, D), jnp.float32).at[flat_ids].add(
        weighted.reshape(EXPERTS * ROWS, D).astype(jnp.float32)).astype(jnp.bfloat16)
    token_grad = jnp.zeros((TOKENS, D), jnp.float32).at[flat_ids].add(
        rows_back.reshape(EXPERTS * ROWS, D).astype(jnp.float32)).astype(jnp.bfloat16)
    gate_grad = jnp.transpose(gate_dots.reshape(EXPERTS, N_EXPERT, PAIR), (1, 0, 2))
    return moe_out, token_grad, gate_grad, grad_gate_w, grad_up_w, grad_down_w
```

```python
import functools

import jax
import jax.numpy as jnp
from jax import lax
from jax.experimental import pallas as pl
from jax.experimental.pallas import tpu as pltpu
from jax.sharding import PartitionSpec as P

BF = jnp.bfloat16
F32 = jnp.float32
LIVE = 256
EMPTY_MARK = 64.0
VMEM_LIMIT = 48 * 1024 * 1024


def dot(a, b):
    return jnp.dot(a, b, preferred_element_type=F32)


def dot_nt(a, b):
    return lax.dot_general(a, b, (((1,), (1,)), ((), ())), preferred_element_type=F32)


def dot_tn(a, b):
    return lax.dot_general(a, b, (((0,), (0,)), ((), ())), preferred_element_type=F32)


def iota(shape, dim):
    return lax.broadcasted_iota(jnp.int32, shape, dim)


def call(kernel, ids, args, outs, flops, scratch=(), blocks=None):
    blocks = blocks or {}
    in_specs = []
    for n, arg in enumerate(args):
        if n in blocks:
            in_specs.append(pl.BlockSpec(*blocks[n]))
        else:
            rank = arg.ndim
            in_specs.append(pl.BlockSpec(arg.shape, lambda i, ids, rank=rank: (0,) * rank))
    out_specs = [
        pl.BlockSpec(shape, lambda i, ids, rank=len(shape): (0,) * rank) for shape, _ in outs
    ]
    moved = sum(a.size * a.dtype.itemsize for a in args)
    moved += sum(functools.reduce(lambda p, q: p * q, s) * jnp.dtype(t).itemsize for s, t in outs)
    return pl.pallas_call(
        kernel,
        out_shape=[jax.ShapeDtypeStruct(s, t) for s, t in outs],
        grid_spec=pltpu.PrefetchScalarGridSpec(
            num_scalar_prefetch=1,
            grid=(1,),
            in_specs=in_specs,
            out_specs=out_specs,
            scratch_shapes=list(scratch),
        ),
        cost_estimate=pl.CostEstimate(flops=flops, bytes_accessed=moved, transcendentals=0),
        compiler_params=pltpu.CompilerParams(vmem_limit_bytes=VMEM_LIMIT),
    )(ids, *args)


def own_expert(array):
    return ((1,) + array.shape[1:], lambda i, ids: (ids[0], 0, 0))


def slot_column(table, core, slots, pair):
    experts = table.shape[0]
    owner = 2 * (iota((slots, experts), 0) // pair) + core
    spread = dot(
        jnp.where(iota((slots, experts), 1) == owner, 1.0, 0.0).astype(BF), table.astype(BF)
    )
    here = iota((slots, pair), 1) == iota((slots, pair), 0) % pair
    return jnp.sum(jnp.where(here, spread, 0.0), axis=1, keepdims=True)


def slot_row(table, core, slots, pair):
    experts = table.shape[0]
    owner = 2 * (iota((experts, slots), 1) // pair) + core
    chosen = jnp.where(iota((experts, slots), 0) == owner, 1.0, 0.0).astype(BF)
    spread = dot_tn(table.astype(BF), chosen)
    here = iota((pair, slots), 0) == iota((pair, slots), 1) % pair
    return jnp.sum(jnp.where(here, spread, 0.0), axis=0, keepdims=True)


def pick_tokens(ids, slot_ref, own_ref, other_ref, sent_ref):
    slots, pair = sent_ref.shape[0], slot_ref.shape[1]
    width = own_ref.shape[1]
    token = slot_column(slot_ref[...].astype(F32), ids[0], slots, pair)
    count = own_ref.shape[0]
    picker = jnp.where(iota((slots, count), 1).astype(F32) == token, 1.0, 0.0).astype(BF)
    empty = token < 0.0
    sent_ref[:, :width] = jnp.where(empty, EMPTY_MARK, dot(picker, own_ref[...])).astype(BF)
    sent_ref[:, width:] = jnp.where(empty, EMPTY_MARK, dot(picker, other_ref[...])).astype(BF)


def pick_grads(ids, slot_ref, gate_ref, own_ref, other_ref, sent_ref):
    slots, pair = sent_ref.shape[0], slot_ref.shape[1]
    width = own_ref.shape[1]
    token = slot_column(slot_ref[...].astype(F32), ids[0], slots, pair)
    gate = slot_column(gate_ref[...].astype(F32), ids[0], slots, pair)
    count = own_ref.shape[0]
    picker = jnp.where(iota((slots, count), 1).astype(F32) == token, 1.0, 0.0).astype(BF)
    sent_ref[:, :width] = (gate * dot(picker, own_ref[...])).astype(BF)
    sent_ref[:, width:] = (gate * dot(picker, other_ref[...])).astype(BF)


def send_chunks(ids, total_ref, own_ref, send_refs):
    chunk = own_ref.shape[0]
    parts = total_ref.shape[0] // chunk
    for k, ref in enumerate((own_ref, *send_refs)):
        at = pl.multiple_of(((ids[1] + k) % parts) * chunk, chunk)
        ref[...] = total_ref[pl.ds(at, chunk), :].astype(ref.dtype)


def forward_in(ids, got_ref, wg_ref, wu_ref, wo_g_ref, wo_u_ref,
               rows_ref, narrow_ref, widen_ref, own_ref, s1, s2, s3, total_ref):
    slots, both = got_ref.shape
    width, hidden = wg_ref.shape[1], wg_ref.shape[2]
    live_rows = rows_ref.shape[0]
    probe = got_ref[:, :128]
    lane0 = jnp.where(iota((8, 128), 1) == 0, 1.0, 0.0).astype(BF)
    live_row = dot_nt(lane0, probe) < EMPTY_MARK / 2
    before = iota((slots, slots), 0) <= iota((slots, slots), 1)
    place_row = dot(
        jnp.where(live_row, 1.0, 0.0).astype(BF), jnp.where(before, 1.0, 0.0).astype(BF)
    )
    place_row = jnp.where(live_row, place_row - 1.0, -1.0)[:1, :]
    narrow = jnp.where(iota((live_rows, slots), 0).astype(F32) == place_row, 1.0, 0.0).astype(BF)
    narrow_ref[...] = narrow
    lane0 = jnp.where(iota((128, 128), 0) == 0, 1.0, 0.0).astype(BF)
    live_col = dot(probe, lane0) < EMPTY_MARK / 2
    after = iota((slots, slots), 0) >= iota((slots, slots), 1)
    place_col = dot(
        jnp.where(after, 1.0, 0.0).astype(BF), jnp.where(live_col, 1.0, 0.0).astype(BF)
    )
    place_col = jnp.where(live_col, place_col - 1.0, -1.0)[:, :1]
    widen_ref[...] = jnp.where(
        iota((slots, live_rows), 1).astype(F32) == place_col, 1.0, 0.0
    ).astype(BF)
    rows_ref[...] = dot(narrow, got_ref[...]).astype(BF)
    mine = rows_ref[:, :width]
    other = rows_ref[:, width:]
    total_ref[:, :hidden] = dot(mine, wg_ref[0]) + dot(other, wo_g_ref[...])
    total_ref[:, hidden:] = dot(mine, wu_ref[0]) + dot(other, wo_u_ref[...])
    send_chunks(ids, total_ref, own_ref, (s1, s2, s3))


def activate(ids, own_ref, r1, r2, r3, pre_ref, hidden_ref):
    hidden = hidden_ref.shape[1]
    pre = own_ref[...] + r1[...].astype(F32) + r2[...].astype(F32) + r3[...].astype(F32)
    pre_ref[...] = pre
    gate_pre = pre[:, :hidden]
    hidden_ref[...] = (jax.nn.silu(gate_pre) * pre[:, hidden:]).astype(BF)


def gather_chunks(ids, refs, whole_ref):
    chunk = refs[0].shape[0]
    parts = whole_ref.shape[0] // chunk
    for k, ref in enumerate(refs):
        at = pl.multiple_of(((ids[1] + parts - k) % parts) * chunk, chunk)
        whole_ref[pl.ds(at, chunk), :] = ref[...]


def forward_out(ids, h0, h1, h2, h3, wd_ref, wo_d_ref, widen_ref, hidden_ref, sent_ref):
    gather_chunks(ids, (h0, h1, h2, h3), hidden_ref)
    width = wd_ref.shape[2]
    hidden = hidden_ref[...]
    widen = widen_ref[...]
    sent_ref[:, :width] = dot(widen, dot(hidden, wd_ref[0]).astype(BF)).astype(BF)
    sent_ref[:, width:] = dot(widen, dot(hidden, wo_d_ref[...]).astype(BF)).astype(BF)


def backward_in(ids, got_ref, narrow_ref, wd_ref, wo_d_ref, rows_ref, own_ref, s1, s2, s3,
                total_ref):
    width = wd_ref.shape[2]
    rows_ref[...] = dot(narrow_ref[...], got_ref[...]).astype(BF)
    total_ref[...] = dot_nt(rows_ref[:, :width], wd_ref[0]) + dot_nt(
        rows_ref[:, width:], wo_d_ref[...]
    )
    send_chunks(ids, total_ref, own_ref, (s1, s2, s3))


def deactivate(ids, own_ref, r1, r2, r3, pre_ref, out_ref):
    hidden = own_ref.shape[1]
    grad = own_ref[...] + r1[...].astype(F32) + r2[...].astype(F32) + r3[...].astype(F32)
    gate_pre = pre_ref[:, :hidden]
    up_pre = pre_ref[:, hidden:]
    sigma = jax.nn.sigmoid(gate_pre)
    slope = sigma * (1.0 + gate_pre * (1.0 - sigma))
    out_ref[:, :hidden] = (grad * up_pre * slope).astype(BF)
    out_ref[:, hidden:] = (grad * (gate_pre * sigma)).astype(BF)


def backward_out(ids, g0, g1, g2, g3, wg_ref, wu_ref, wo_g_ref, wo_u_ref, widen_ref,
                 grads_ref, sent_ref):
    gather_chunks(ids, (g0, g1, g2, g3), grads_ref)
    width, hidden = wg_ref.shape[1], wg_ref.shape[2]
    gate = grads_ref[:, :hidden]
    up = grads_ref[:, hidden:]
    widen = widen_ref[...]
    back = dot_nt(gate, wg_ref[0]) + dot_nt(up, wu_ref[0])
    sent_ref[:, :width] = dot(widen, back.astype(BF)).astype(BF)
    back = dot_nt(gate, wo_g_ref[...]) + dot_nt(up, wo_u_ref[...])
    sent_ref[:, width:] = dot(widen, back.astype(BF)).astype(BF)


def combine_out(ids, back_ref, slot_ref, gate_ref, own_ref, other_ref, mine_ref, theirs_ref,
                dots_ref):
    slots, both = back_ref.shape
    count, width = own_ref.shape
    pair = slot_ref.shape[1]
    slot_table = slot_ref[...].astype(F32)
    token_row = slot_row(slot_table, ids[0], slots, pair)
    gate_row = slot_row(gate_ref[...].astype(F32), ids[0], slots, pair)
    adder = jnp.where(
        iota((count, slots), 0).astype(F32) == token_row, gate_row, 0.0
    ).astype(BF)
    mine_ref[...] = dot(adder, back_ref[:, :width])
    theirs_ref[...] = dot(adder, back_ref[:, width:])
    token = slot_column(slot_table, ids[0], slots, pair)
    picker = jnp.where(iota((slots, count), 1).astype(F32) == token, 1.0, 0.0).astype(BF)
    terms = dot(picker, own_ref[...]) * back_ref[:, :width].astype(F32)
    terms = terms + dot(picker, other_ref[...]) * back_ref[:, width:].astype(F32)
    sums = jnp.sum(terms, axis=1, keepdims=True)
    here = iota((slots, pair), 1) == iota((slots, pair), 0) % pair
    spread = jnp.where(here, sums, 0.0)
    dots_ref[...] = jnp.sum(spread.reshape(slots // pair, pair, pair), axis=1)


def combine_back(ids, back_ref, slot_ref, mine_ref, theirs_ref):
    slots, both = back_ref.shape
    count, width = mine_ref.shape
    pair = slot_ref.shape[1]
    token_row = slot_row(slot_ref[...].astype(F32), ids[0], slots, pair)
    adder = jnp.where(iota((count, slots), 0).astype(F32) == token_row, 1.0, 0.0).astype(BF)
    mine_ref[...] = dot(adder, back_ref[:, :width])
    theirs_ref[...] = dot(adder, back_ref[:, width:])


def local(tokens, out_grad, slot_token, slot_gate, w_gate, w_up, w_down):
    senders = lax.axis_size("expert")
    devices = lax.axis_size("dp")
    parts = devices // 2
    count, width = tokens.shape
    both = 2 * width
    experts, pair = slot_token.shape[1:]
    hidden = w_gate.shape[2]
    slots = senders * pair
    chunk = LIVE // parts
    place = lax.axis_index("dp")
    core = place % 2
    ids = jnp.stack([core, place // 2]).astype(jnp.int32)
    slot_table = slot_token[0]
    gate_table = slot_gate[0]

    def swap(value):
        return lax.ppermute(value, "dp", [(i, i ^ 1) for i in range(devices)])

    def along(value, k):
        return lax.ppermute(value, "dp", [(i, (i + 2 * k) % devices) for i in range(devices)])

    def exchange(value):
        value = value.reshape(senders, pair, both)
        value = lax.all_to_all(value, "expert", split_axis=0, concat_axis=0, tiled=True)
        return value.reshape(slots, both)

    def of_other(value):
        return lax.dynamic_index_in_dim(value, 1 - core, 0, keepdims=False)

    tok_other = swap(tokens)
    grad_other = swap(out_grad)
    wo_g = swap(of_other(w_gate))
    wo_u = swap(of_other(w_up))
    wo_d = swap(of_other(w_down))
    picks = 4 * slots * count * width
    move = 4 * LIVE * slots * width
    mm = 4 * LIVE * width * hidden

    (sent_in,) = call(pick_tokens, ids, (slot_table, tokens, tok_other), [((slots, both), BF)], picks)
    got_in = exchange(sent_in)
    (sent_grad,) = call(
        pick_grads, ids, (slot_table, gate_table, out_grad, grad_other), [((slots, both), BF)], picks
    )
    got_grad = exchange(sent_grad)

    rows_in, narrow, widen, own, *sends = call(
        forward_in,
        ids,
        (got_in, w_gate, w_up, wo_g, wo_u),
        [((LIVE, both), BF), ((LIVE, slots), BF), ((slots, LIVE), BF), ((chunk, 2 * hidden), F32)]
        + [((chunk, 2 * hidden), BF)] * 3,
        move + 2 * mm,
        scratch=[pltpu.VMEM((LIVE, 2 * hidden), F32)],
        blocks={1: own_expert(w_gate), 2: own_expert(w_up)},
    )
    sums = [along(value, k + 1) for k, value in enumerate(sends)]
    pre, hidden_own = call(
        activate, ids, (own, *sums), [((chunk, 2 * hidden), F32), ((chunk, hidden), BF)],
        8 * chunk * hidden,
    )
    hidden_all, sent_out = call(
        forward_out,
        ids,
        (hidden_own, *[along(hidden_own, k) for k in range(1, parts)], w_down, wo_d, widen),
        [((LIVE, hidden), BF), ((slots, both), BF)],
        move + mm,
        blocks={parts: own_expert(w_down)},
    )
    back_out = exchange(sent_out)

    rows_grad, own, *sends = call(
        backward_in,
        ids,
        (got_grad, narrow, w_down, wo_d),
        [((LIVE, both), BF), ((chunk, hidden), F32)] + [((chunk, hidden), BF)] * 3,
        move + mm,
        scratch=[pltpu.VMEM((LIVE, hidden), F32)],
        blocks={2: own_expert(w_down)},
    )
    sums = [along(value, k + 1) for k, value in enumerate(sends)]
    (pre_grads,) = call(
        deactivate, ids, (own, *sums, pre), [((chunk, 2 * hidden), BF)], 12 * chunk * hidden
    )
    grads_all, sent_back = call(
        backward_out,
        ids,
        (pre_grads, *[along(pre_grads, k) for k in range(1, parts)], w_gate, w_up, wo_g, wo_u, widen),
        [((LIVE, 2 * hidden), BF), ((slots, both), BF)],
        move + 2 * mm,
        blocks={parts: own_expert(w_gate), parts + 1: own_expert(w_up)},
    )
    back_grad = exchange(sent_back)

    out_mine, out_theirs, dots = call(
        combine_out,
        ids,
        (back_out, slot_table, gate_table, out_grad, grad_other),
        [((count, width), F32), ((count, width), F32), ((senders, pair), F32)],
        2 * picks,
    )
    moe_out = (out_mine + swap(out_theirs)).astype(BF)
    dots = dots + along(dots, 1) + along(dots, 2) + along(dots, 3)
    dots = dots.astype(BF)
    dots_other = swap(dots)
    gate_grad = jnp.where(
        core == 0, jnp.stack([dots, dots_other], 1), jnp.stack([dots_other, dots], 1)
    ).reshape(1, experts, pair)

    def place_pair(mine, other):
        return jnp.where(core == 0, jnp.stack([mine, other]), jnp.stack([other, mine]))

    grad_in = dot_tn(rows_in, grads_all).astype(BF)
    grad_in_mine = grad_in[:width]
    grad_in_other = swap(grad_in[width:])
    grad_gate_w = place_pair(grad_in_mine[:, :hidden], grad_in_other[:, :hidden])
    grad_up_w = place_pair(grad_in_mine[:, hidden:], grad_in_other[:, hidden:])
    grad_down_mine = dot_tn(hidden_all, rows_grad[:, :width]).astype(BF)
    grad_down_other = swap(dot_tn(hidden_all, rows_grad[:, width:]).astype(BF))
    grad_down_w = place_pair(grad_down_mine, grad_down_other)

    tok_mine, tok_theirs = call(
        combine_back,
        ids,
        (back_grad, slot_table),
        [((count, width), F32), ((count, width), F32)],
        picks,
    )
    token_grad = (tok_mine + swap(tok_theirs)).astype(BF)
    return (moe_out, token_grad, gate_grad, grad_gate_w, grad_up_w, grad_down_w)


def solution(mesh):
    placed = (
        P("expert", "dp"),
        P("expert", "dp"),
        P("expert", None, None),
        P("expert", None, None),
        P("expert", "dp", None),
        P("expert", "dp", None),
        P("expert", None, "dp"),
    )
    return jax.shard_map(
        local,
        mesh=mesh,
        in_specs=placed,
        out_specs=(
            P("expert", "dp"),
            P("expert", "dp"),
            P("expert", None, None),
            P("expert", "dp", None),
            P("expert", "dp", None),
            P("expert", None, "dp"),
        ),
        check_vma=False,
    )
```

```python
import functools

import jax
import jax.numpy as jnp
from jax import lax
from jax.experimental import pallas as pl
from jax.experimental.pallas import tpu as pltpu
from jax.sharding import PartitionSpec as P

BF = jnp.bfloat16
F32 = jnp.float32
LIVE = 256
EMPTY_MARK = 64.0
VMEM_LIMIT = 24 * 1024 * 1024


def dot(a, b):
    return jnp.dot(a, b, preferred_element_type=F32)


def dot_nt(a, b):
    return lax.dot_general(a, b, (((1,), (1,)), ((), ())), preferred_element_type=F32)


def dot_tn(a, b):
    return lax.dot_general(a, b, (((0,), (0,)), ((), ())), preferred_element_type=F32)


def iota(shape, dim):
    return lax.broadcasted_iota(jnp.int32, shape, dim)


IN_VMEM = pl.BlockSpec(memory_space=pltpu.VMEM)
IN_HBM = pl.BlockSpec(memory_space=pltpu.HBM)


def call(kernel, ids, args, outs, flops, scratch=(), placed=(), left=(), aliases=()):
    moved = sum(a.size * a.dtype.itemsize for a in args)
    moved += sum(functools.reduce(lambda p, q: p * q, s) * jnp.dtype(t).itemsize for s, t in outs)
    args = [
        pltpu.with_memory_space_constraint(a, pltpu.HBM) if n in left else a
        for n, a in enumerate(args)
    ]
    return pl.pallas_call(
        kernel,
        out_shape=[
            pltpu.HBM(s, t) if n in placed else jax.ShapeDtypeStruct(s, t)
            for n, (s, t) in enumerate(outs)
        ],
        in_specs=[pl.BlockSpec(memory_space=pltpu.SMEM)]
        + [IN_HBM if n in left else IN_VMEM for n in range(len(args))],
        out_specs=[IN_HBM if n in placed else IN_VMEM for n in range(len(outs))],
        scratch_shapes=list(scratch),
        input_output_aliases={n + 1: m for n, m in aliases},
        cost_estimate=pl.CostEstimate(flops=flops, bytes_accessed=moved, transcendentals=0),
        compiler_params=pltpu.CompilerParams(vmem_limit_bytes=VMEM_LIMIT),
    )(ids, *args)


def slot_column(table, core, slots):
    pair, experts = table.shape
    owner = 2 * (iota((slots, experts), 0) // pair) + core
    spread = dot_nt(
        jnp.where(iota((slots, experts), 1) == owner, 1.0, 0.0).astype(BF), table.astype(BF)
    )
    here = iota((slots, pair), 1) == iota((slots, pair), 0) % pair
    return jnp.sum(jnp.where(here, spread, 0.0), axis=1, keepdims=True)


def slot_row(table, core, slots):
    pair, experts = table.shape
    owner = 2 * (iota((experts, slots), 1) // pair) + core
    chosen = jnp.where(iota((experts, slots), 0) == owner, 1.0, 0.0).astype(BF)
    spread = dot(table.astype(BF), chosen)
    here = iota((pair, slots), 0) == iota((pair, slots), 1) % pair
    return jnp.sum(jnp.where(here, spread, 0.0), axis=0, keepdims=True)


def row_picker(slot_ref, ids, slots, count):
    token = slot_column(slot_ref[...].astype(F32), ids[0], slots)
    picker = jnp.where(iota((slots, count), 1).astype(F32) == token, 1.0, 0.0).astype(BF)
    return token, picker


def started(source, target, sem):
    copy = pltpu.make_async_copy(source, target, sem)
    copy.start()
    return copy


def leave_blocks(blocks, buffer, out_ref, sems):
    width = buffer.shape[1] // len(blocks)
    copies = []
    for n, half in enumerate(blocks):
        at = pl.ds(n * width, width)
        buffer[:, at] = half()
        copies.append(started(buffer.at[:, at], out_ref.at[:, at], sems.at[n]))
    for copy in copies:
        copy.wait()


def pick_tokens(ids, slot_hbm, own_hbm, other_ref, sent_ref, buffer, sems, slot_ref, own_ref, in_sems):
    slots, both = sent_ref.shape
    slot_in = started(slot_hbm, slot_ref, in_sems.at[0])
    own_in = started(own_hbm, own_ref, in_sems.at[1])
    slot_in.wait()
    token, picker = row_picker(slot_ref, ids, slots, own_ref.shape[0])
    empty = token < 0.0
    own_in.wait()
    leave_blocks(
        [
            lambda ref=ref: jnp.where(empty, EMPTY_MARK, dot(picker, ref[...])).astype(BF)
            for ref in (own_ref, other_ref)
        ],
        buffer, sent_ref, sems,
    )


def pick_grads(ids, slot_ref, gate_ref, own_ref, other_ref, sent_ref, buffer, sems):
    slots, both = sent_ref.shape
    token, picker = row_picker(slot_ref, ids, slots, own_ref.shape[0])
    gate = slot_column(gate_ref[...].astype(F32), ids[0], slots)
    leave_blocks(
        [
            lambda ref=ref: (gate * dot(picker, ref[...])).astype(BF)
            for ref in (own_ref, other_ref)
        ],
        buffer, sent_ref, sems,
    )


def send_chunks(ids, total_ref, own_ref, send_refs):
    chunk = own_ref.shape[0]
    parts = total_ref.shape[0] // chunk
    for k, ref in enumerate((own_ref, *send_refs)):
        at = pl.multiple_of(((ids[1] + k) % parts) * chunk, chunk)
        ref[...] = total_ref[pl.ds(at, chunk), :].astype(ref.dtype)


def join_chunks(ids, refs, whole_ref):
    chunk = refs[0].shape[0]
    parts = whole_ref.shape[0] // chunk
    for k, ref in enumerate(refs):
        at = pl.multiple_of(((ids[1] + parts - k) % parts) * chunk, chunk)
        whole_ref[pl.ds(at, chunk), :] = ref[...]


def forward_in(ids, got_hbm, wo_u_hbm, wg_ref, wu_ref, wo_g_ref,
               rows_hbm, narrow_hbm, widen_hbm, own_ref, s1, s2, s3,
               total_ref, got_ref, rows_ref, narrow_ref, widen_ref, wo_u_ref, sems):
    slots, both = got_ref.shape
    width, hidden = wg_ref.shape
    live_rows = rows_ref.shape[0]
    first, rest = pl.ds(0, 128), pl.ds(128, both - 128)
    first_in = started(got_hbm.at[:, first], got_ref.at[:, first], sems.at[0])
    rest_in = started(got_hbm.at[:, rest], got_ref.at[:, rest], sems.at[1])
    wo_u_in = started(wo_u_hbm, wo_u_ref, sems.at[5])
    first_in.wait()
    probe = got_ref[:, :128]
    lane0 = jnp.where(iota((8, 128), 1) == 0, 1.0, 0.0).astype(BF)
    live_row = dot_nt(lane0, probe) < EMPTY_MARK / 2
    before = iota((slots, slots), 0) <= iota((slots, slots), 1)
    place_row = dot(
        jnp.where(live_row, 1.0, 0.0).astype(BF), jnp.where(before, 1.0, 0.0).astype(BF)
    )
    place_row = jnp.where(live_row, place_row - 1.0, -1.0)[:1, :]
    narrow = jnp.where(iota((live_rows, slots), 0).astype(F32) == place_row, 1.0, 0.0).astype(BF)
    narrow_ref[...] = narrow
    narrow_out = started(narrow_ref, narrow_hbm, sems.at[2])
    rest_in.wait()
    rows_ref[...] = dot(narrow, got_ref[...]).astype(BF)
    rows_out = started(rows_ref, rows_hbm, sems.at[3])
    mine = rows_ref[:, :width]
    other = rows_ref[:, width:]
    total_ref[:, :hidden] = dot(mine, wg_ref[...]) + dot(other, wo_g_ref[...])
    wo_u_in.wait()
    total_ref[:, hidden:] = dot(mine, wu_ref[...]) + dot(other, wo_u_ref[...])
    send_chunks(ids, total_ref, own_ref, (s1, s2, s3))
    widen_ref[...] = narrow_ref[...].T
    widen_out = started(widen_ref, widen_hbm, sems.at[4])
    narrow_out.wait()
    rows_out.wait()
    widen_out.wait()


def activate(ids, own_ref, r1, r2, r3, pre_hbm, hidden_ref, pre_ref, sems):
    hidden = hidden_ref.shape[1]
    pre = own_ref[...] + r1[...].astype(F32) + r2[...].astype(F32) + r3[...].astype(F32)
    pre_ref[...] = pre
    pre_out = started(pre_ref, pre_hbm, sems.at[0])
    hidden_ref[...] = (jax.nn.silu(pre[:, :hidden]) * pre[:, hidden:]).astype(BF)
    pre_out.wait()


def forward_out(ids, h0, h1, h2, h3, wd_ref, wo_d_ref, widen_hbm, hidden_hbm, sent_ref, buffer,
                sems, hidden_ref, widen_ref, more_sems):
    widen_in = started(widen_hbm, widen_ref, more_sems.at[1])
    join_chunks(ids, (h0, h1, h2, h3), hidden_ref)
    hidden_out = started(hidden_ref, hidden_hbm, more_sems.at[0])
    width = wd_ref.shape[1]
    out = [dot(hidden_ref[...], ref[...]).astype(BF) for ref in (wd_ref, wo_d_ref)]
    widen_in.wait()
    leave_blocks(
        [
            lambda half=half, at=at: dot(widen_ref[...], half[:, at : at + width // 2]).astype(BF)
            for half in out
            for at in (0, width // 2)
        ],
        buffer, sent_ref, sems,
    )
    hidden_out.wait()


def backward_in(ids, got_hbm, narrow_hbm, wd_hbm, wo_d_hbm, rows_hbm, own_ref, s1, s2, s3,
                total_ref, got_ref, narrow_ref, wd_ref, wo_d_ref, rows_ref, sems):
    width = wd_ref.shape[1]
    narrow_in = started(narrow_hbm, narrow_ref, sems.at[0])
    mine, other = pl.ds(0, width), pl.ds(width, width)
    mine_in = started(got_hbm.at[:, mine], got_ref.at[:, mine], sems.at[1])
    other_in = started(got_hbm.at[:, other], got_ref.at[:, other], sems.at[2])
    wd_in = started(wd_hbm, wd_ref, sems.at[3])
    wo_d_in = started(wo_d_hbm, wo_d_ref, sems.at[4])
    narrow_in.wait()
    mine_in.wait()
    rows_ref[:, :width] = dot(narrow_ref[...], got_ref[:, :width]).astype(BF)
    other_in.wait()
    rows_ref[:, width:] = dot(narrow_ref[...], got_ref[:, width:]).astype(BF)
    rows_out = started(rows_ref, rows_hbm, sems.at[5])
    wd_in.wait()
    total_ref[...] = dot_nt(rows_ref[:, :width], wd_ref[...])
    wo_d_in.wait()
    total_ref[...] += dot_nt(rows_ref[:, width:], wo_d_ref[...])
    send_chunks(ids, total_ref, own_ref, (s1, s2, s3))
    rows_out.wait()


def deactivate(ids, own_ref, r1, r2, r3, pre_ref, out_ref):
    hidden = own_ref.shape[1]
    grad = own_ref[...] + r1[...].astype(F32) + r2[...].astype(F32) + r3[...].astype(F32)
    gate_pre = pre_ref[:, :hidden]
    up_pre = pre_ref[:, hidden:]
    sigma = jax.nn.sigmoid(gate_pre)
    slope = sigma * (1.0 + gate_pre * (1.0 - sigma))
    out_ref[:, :hidden] = (grad * up_pre * slope).astype(BF)
    out_ref[:, hidden:] = (grad * (gate_pre * sigma)).astype(BF)


def backward_out(ids, g0, g1, g2, g3, wg_ref, wu_ref, wo_g_ref, wo_u_ref, widen_ref,
                 grads_hbm, sent_ref, buffer, sems, grads_ref, grads_sems):
    join_chunks(ids, (g0, g1, g2, g3), grads_ref)
    grads_out = started(grads_ref, grads_hbm, grads_sems.at[0])
    hidden = wg_ref.shape[1]
    gate = grads_ref[:, :hidden]
    up = grads_ref[:, hidden:]
    widen = widen_ref[...]

    def half(gate_w, up_w):
        back = dot_nt(gate, gate_w[...]) + dot_nt(up, up_w[...])
        return dot(widen, back.astype(BF)).astype(BF)

    leave_blocks(
        [lambda: half(wg_ref, wu_ref), lambda: half(wo_g_ref, wo_u_ref)], buffer, sent_ref, sems
    )
    grads_out.wait()


def combine_out(ids, back_hbm, own_hbm, other_hbm, slot_ref, gate_ref, mine_ref, theirs_ref,
                dots_ref, back_ref, own_ref, other_ref, sems):
    slots, both = back_ref.shape
    count, width = own_ref.shape
    pair = slot_ref.shape[0]
    mine, other = pl.ds(0, width), pl.ds(width, width)
    back_mine = started(back_hbm.at[:, mine], back_ref.at[:, mine], sems.at[0])
    own_in = started(own_hbm, own_ref, sems.at[1])
    back_other = started(back_hbm.at[:, other], back_ref.at[:, other], sems.at[2])
    other_in = started(other_hbm, other_ref, sems.at[3])
    token_row = slot_row(slot_ref[...].astype(F32), ids[0], slots)
    gate_row = slot_row(gate_ref[...].astype(F32), ids[0], slots)
    adder = jnp.where(
        iota((count, slots), 0).astype(F32) == token_row, gate_row, 0.0
    ).astype(BF)
    token, picker = row_picker(slot_ref, ids, slots, count)
    back_mine.wait()
    mine_ref[...] = dot(adder, back_ref[:, :width])
    own_in.wait()
    sums = jnp.sum(
        dot(picker, own_ref[...]) * back_ref[:, :width].astype(F32), axis=1, keepdims=True
    )
    back_other.wait()
    theirs_ref[...] = dot(adder, back_ref[:, width:])
    other_in.wait()
    sums = sums + jnp.sum(
        dot(picker, other_ref[...]) * back_ref[:, width:].astype(F32), axis=1, keepdims=True
    )
    here = iota((slots, pair), 1) == iota((slots, pair), 0) % pair
    spread = jnp.where(here, sums, 0.0)
    dots_ref[...] = jnp.sum(spread.reshape(slots // pair, pair, pair), axis=1)


def adder_of(ids, slot_ref, count, slots):
    token_row = slot_row(slot_ref[...].astype(F32), ids[0], slots)
    return jnp.where(iota((count, slots), 0).astype(F32) == token_row, 1.0, 0.0).astype(BF)


def combine_theirs(ids, back_ref, slot_ref, theirs_ref):
    count, width = theirs_ref.shape
    adder = adder_of(ids, slot_ref, count, back_ref.shape[0])
    theirs_ref[...] = dot(adder, back_ref[:, width:])


def combine_mine(ids, back_ref, slot_ref, mine_ref):
    count, width = mine_ref.shape
    adder = adder_of(ids, slot_ref, count, back_ref.shape[0])
    mine_ref[...] = dot(adder, back_ref[:, :width])


def add_halves(ids, mine_ref, got_ref, out_ref):
    out_ref[...] = (mine_ref[...] + got_ref[...]).astype(BF)


def load_rows(rows_in_hbm, grads_hbm, hidden_hbm, rows_grad_hbm, at, refs, sems):
    sources = (rows_in_hbm.at[:, at], grads_hbm, rows_grad_hbm.at[:, at], hidden_hbm)
    return [started(source, ref, sems.at[n]) for n, (source, ref) in enumerate(zip(sources, refs))]


def weights_theirs(ids, rows_in_hbm, grads_hbm, hidden_hbm, rows_grad_hbm, in_ref, down_ref,
                   rows_in_ref, grads_ref, rows_grad_ref, hidden_ref, sems):
    width = in_ref.shape[0]
    loads = load_rows(rows_in_hbm, grads_hbm, hidden_hbm, rows_grad_hbm, pl.ds(width, width),
                      (rows_in_ref, grads_ref, rows_grad_ref, hidden_ref), sems)
    loads[0].wait()
    loads[1].wait()
    in_ref[...] = dot_tn(rows_in_ref[...], grads_ref[...]).astype(BF)
    loads[2].wait()
    loads[3].wait()
    down_ref[...] = dot_tn(hidden_ref[...], rows_grad_ref[...]).astype(BF)


def weights_mine(ids, rows_in_hbm, grads_hbm, hidden_hbm, rows_grad_hbm, gate_ref, up_ref, down_ref,
                 rows_in_ref, grads_ref, rows_grad_ref, hidden_ref, mine_in, mine_down, sems):
    width, hidden = gate_ref.shape[1:]
    core = ids[0]
    loads = load_rows(rows_in_hbm, grads_hbm, hidden_hbm, rows_grad_hbm, pl.ds(0, width),
                      (rows_in_ref, grads_ref, rows_grad_ref, hidden_ref), sems)
    loads[0].wait()
    loads[1].wait()
    mine_in[...] = dot_tn(rows_in_ref[...], grads_ref[...]).astype(BF)
    stores = [
        started(mine_in.at[:, pl.ds(0, hidden)], gate_ref.at[core], sems.at[4]),
        started(mine_in.at[:, pl.ds(hidden, hidden)], up_ref.at[core], sems.at[5]),
    ]
    loads[2].wait()
    loads[3].wait()
    mine_down[...] = dot_tn(hidden_ref[...], rows_grad_ref[...]).astype(BF)
    stores.append(started(mine_down, down_ref.at[core], sems.at[6]))
    for store in stores:
        store.wait()


def weights_got(ids, got_in_ref, got_down_ref, gate_in, up_in, down_in, gate_ref, up_ref, down_ref,
                sems):
    hidden = gate_ref.shape[2]
    there = 1 - ids[0]
    stores = [
        started(got_in_ref.at[:, pl.ds(0, hidden)], gate_ref.at[there], sems.at[0]),
        started(got_in_ref.at[:, pl.ds(hidden, hidden)], up_ref.at[there], sems.at[1]),
        started(got_down_ref, down_ref.at[there], sems.at[2]),
    ]
    for store in stores:
        store.wait()


def local(tokens, out_grad, slot_token, slot_gate, w_gate, w_up, w_down):
    senders = lax.axis_size("expert")
    devices = lax.axis_size("dp")
    parts = devices // 2
    count, width = tokens.shape
    both = 2 * width
    experts, pair = slot_token.shape[1:]
    hidden = w_gate.shape[2]
    slots = senders * pair
    chunk = LIVE // parts
    place = lax.axis_index("dp")
    core = place % 2
    ids = jnp.stack([core, place // 2]).astype(jnp.int32)
    slot_table = slot_token[0].T
    gate_table = slot_gate[0].T

    def swap(value):
        return lax.ppermute(value, "dp", [(i, i ^ 1) for i in range(devices)])

    def along(value, k):
        return lax.ppermute(value, "dp", [(i, (i + 2 * k) % devices) for i in range(devices)])

    def spread(values):
        return [along(value, k + 1) for k, value in enumerate(values)]

    def gather_x(value):
        return [value] + spread([value] * (parts - 1))

    def exchange(value):
        value = value.reshape(senders, pair, both)
        value = lax.all_to_all(value, "expert", split_axis=0, concat_axis=0, tiled=True)
        return value.reshape(slots, both)

    def pick_expert(value, which):
        return lax.dynamic_index_in_dim(value, which, 0, keepdims=False)

    tok_other = swap(tokens)
    grad_other = swap(out_grad)
    wg, wu, wd = (pick_expert(w, core) for w in (w_gate, w_up, w_down))
    wo_g, wo_u, wo_d = (swap(pick_expert(w, 1 - core)) for w in (w_gate, w_up, w_down))
    picks = 4 * slots * count * width
    move = 4 * LIVE * slots * width
    mm = 4 * LIVE * width * hidden
    sent = ((slots, both), BF)
    buffers = [pltpu.VMEM((slots, both), BF), pltpu.SemaphoreType.DMA((4,))]

    def room(*shapes):
        return [pltpu.VMEM(shape, dtype) for shape, dtype in shapes]

    def sems(n):
        return [pltpu.SemaphoreType.DMA((n,))]

    (sent_in,) = call(
        pick_tokens, ids, (slot_table, tokens, tok_other), [sent], picks,
        buffers + room((slot_table.shape, jnp.int32), (tokens.shape, BF)) + sems(2), (0,), (0, 1),
    )
    got_in = exchange(sent_in)
    (sent_grad,) = call(
        pick_grads, ids, (slot_table, gate_table, out_grad, grad_other), [sent], picks, buffers, (0,)
    )
    sent_grad, wg, wu, wd, wo_g, wo_u, wo_d = lax.optimization_barrier(
        (sent_grad, wg, wu, wd, wo_g, wo_u, wo_d)
    )
    got_grad = exchange(sent_grad)

    rows_in, narrow, widen, own, *sends = call(
        forward_in,
        ids,
        (got_in, wo_u, wg, wu, wo_g),
        [
            ((LIVE, both), BF),
            ((LIVE, slots), BF),
            ((slots, LIVE), BF),
            ((chunk, 2 * hidden), F32),
        ]
        + [((chunk, 2 * hidden), BF)] * (parts - 1),
        move + 2 * mm,
        room(
            ((LIVE, 2 * hidden), F32),
            ((slots, both), BF),
            ((LIVE, both), BF),
            ((LIVE, slots), BF),
            ((slots, LIVE), BF),
            ((width, hidden), BF),
        )
        + sems(6),
        (0, 1, 2),
        (0, 1),
    )
    pre, hidden_own = call(
        activate,
        ids,
        (own, *spread(sends)),
        [((chunk, 2 * hidden), F32), ((chunk, hidden), BF)],
        8 * chunk * hidden,
        room(((chunk, 2 * hidden), F32)) + sems(1),
        (0,),
    )
    hidden_all, sent_out = call(
        forward_out,
        ids,
        (*gather_x(hidden_own), wd, wo_d, widen),
        [((LIVE, hidden), BF), sent],
        move + mm,
        buffers + room(((LIVE, hidden), BF), ((slots, LIVE), BF)) + sems(2),
        (0, 1),
        (parts + 2,),
    )
    back_out = exchange(sent_out)

    rows_grad, own, *sends = call(
        backward_in,
        ids,
        (got_grad, narrow, wd, wo_d),
        [((LIVE, both), BF), ((chunk, hidden), F32)] + [((chunk, hidden), BF)] * (parts - 1),
        move + mm,
        room(
            ((LIVE, hidden), F32),
            ((slots, both), BF),
            ((LIVE, slots), BF),
            ((hidden, width), BF),
            ((hidden, width), BF),
            ((LIVE, both), BF),
        )
        + sems(6),
        (0,),
        (0, 1, 2, 3),
    )
    (pre_grads,) = call(
        deactivate,
        ids,
        (own, *spread(sends), pre),
        [((chunk, 2 * hidden), BF)],
        12 * chunk * hidden,
    )
    grads_all, sent_back = call(
        backward_out,
        ids,
        (*gather_x(pre_grads), wg, wu, wo_g, wo_u, widen),
        [((LIVE, 2 * hidden), BF), sent],
        move + 2 * mm,
        buffers + room(((LIVE, 2 * hidden), BF)) + sems(1),
        (0, 1),
    )
    back_grad = exchange(sent_back)

    out_mine, out_theirs, dots = call(
        combine_out,
        ids,
        (back_out, out_grad, grad_other, slot_table, gate_table),
        [((count, width), F32), ((count, width), F32), ((senders, pair), F32)],
        2 * picks,
        room(((slots, both), BF), ((count, width), BF), ((count, width), BF)) + sems(4),
        (),
        (0, 1, 2),
    )
    rows_in, grads_all, hidden_all, rows_grad, out_theirs, dots = lax.optimization_barrier(
        (rows_in, grads_all, hidden_all, rows_grad, out_theirs, dots)
    )
    rows = (rows_in, grads_all, hidden_all, rows_grad)
    rows_room = room(
        ((LIVE, width), BF), ((LIVE, 2 * hidden), BF), ((LIVE, width), BF), ((LIVE, hidden), BF)
    )
    theirs_in, theirs_down = call(
        weights_theirs,
        ids,
        rows,
        [((width, 2 * hidden), BF), ((hidden, width), BF)],
        3 * mm // 2,
        rows_room + sems(4),
        (),
        (0, 1, 2, 3),
    )
    weight_shapes = [(w_gate.shape, BF), (w_up.shape, BF), (w_down.shape, BF)]
    weight_grads = call(
        weights_mine,
        ids,
        rows,
        weight_shapes,
        3 * mm // 2,
        rows_room + room(((width, 2 * hidden), BF), ((hidden, width), BF)) + sems(7),
        (0, 1, 2),
        (0, 1, 2, 3),
    )
    moe_out = (out_mine + swap(out_theirs)).astype(BF)
    *dots, weight_grads = lax.optimization_barrier((*gather_x(dots), weight_grads))
    dots = sum(dots).astype(BF)
    dots_other = swap(dots)
    gate_grad = jnp.where(
        core == 0, jnp.stack([dots, dots_other], 1), jnp.stack([dots_other, dots], 1)
    ).reshape(1, experts, pair)
    grad_gate_w, grad_up_w, grad_down_w = call(
        weights_got,
        ids,
        (swap(theirs_in), swap(theirs_down), *weight_grads),
        weight_shapes,
        0,
        sems(3),
        (0, 1, 2),
        (2, 3, 4),
        ((2, 0), (3, 1), (4, 2)),
    )
    back_grad, moe_out, gate_grad, grad_gate_w, grad_up_w, grad_down_w = lax.optimization_barrier(
        (back_grad, moe_out, gate_grad, grad_gate_w, grad_up_w, grad_down_w)
    )
    half = [((count, width), F32)]
    (tok_theirs,) = call(combine_theirs, ids, (back_grad, slot_table), half, picks // 2)
    (tok_mine,) = call(combine_mine, ids, (back_grad, slot_table), half, picks // 2)
    (token_grad,) = call(
        add_halves, ids, (tok_mine, swap(tok_theirs)), [((count, width), BF)], count * width
    )
    return (moe_out, token_grad, gate_grad, grad_gate_w, grad_up_w, grad_down_w)


def solution(mesh):
    placed = (
        P("expert", "dp"),
        P("expert", "dp"),
        P("expert", None, None),
        P("expert", None, None),
        P("expert", "dp", None),
        P("expert", "dp", None),
        P("expert", None, "dp"),
    )
    return jax.shard_map(
        local,
        mesh=mesh,
        in_specs=placed,
        out_specs=(
            P("expert", "dp"),
            P("expert", "dp"),
            P("expert", None, None),
            P("expert", "dp", None),
            P("expert", "dp", None),
            P("expert", None, "dp"),
        ),
        check_vma=False,
    )
```

```python
import functools

import jax
import jax.numpy as jnp
from jax import lax
from jax.experimental import pallas as pl
from jax.experimental.pallas import tpu as pltpu
from jax.sharding import PartitionSpec as P

BF = jnp.bfloat16
F32 = jnp.float32
LIVE = 256
EMPTY_MARK = 64.0
VMEM_LIMIT = 24 * 1024 * 1024


def dot(a, b):
    return jnp.dot(a, b, preferred_element_type=F32)


def dot_nt(a, b):
    return lax.dot_general(a, b, (((1,), (1,)), ((), ())), preferred_element_type=F32)


def dot_tn(a, b):
    return lax.dot_general(a, b, (((0,), (0,)), ((), ())), preferred_element_type=F32)


def iota(shape, dim):
    return lax.broadcasted_iota(jnp.int32, shape, dim)


IN_VMEM = pl.BlockSpec(memory_space=pltpu.VMEM)
IN_HBM = pl.BlockSpec(memory_space=pltpu.HBM)


def call(kernel, ids, args, outs, flops, scratch=(), placed=(), left=(), aliases=()):
    moved = sum(a.size * a.dtype.itemsize for a in args)
    moved += sum(functools.reduce(lambda p, q: p * q, s) * jnp.dtype(t).itemsize for s, t in outs)
    args = [
        pltpu.with_memory_space_constraint(a, pltpu.HBM) if n in left else a
        for n, a in enumerate(args)
    ]
    return pl.pallas_call(
        kernel,
        out_shape=[
            pltpu.HBM(s, t) if n in placed else jax.ShapeDtypeStruct(s, t)
            for n, (s, t) in enumerate(outs)
        ],
        in_specs=[pl.BlockSpec(memory_space=pltpu.SMEM)]
        + [IN_HBM if n in left else IN_VMEM for n in range(len(args))],
        out_specs=[IN_HBM if n in placed else IN_VMEM for n in range(len(outs))],
        scratch_shapes=list(scratch),
        input_output_aliases={n + 1: m for n, m in aliases},
        cost_estimate=pl.CostEstimate(flops=flops, bytes_accessed=moved, transcendentals=0),
        compiler_params=pltpu.CompilerParams(vmem_limit_bytes=VMEM_LIMIT),
    )(ids, *args)


def slot_column(table, core, slots):
    pair, experts = table.shape
    owner = 2 * (iota((slots, experts), 0) // pair) + core
    spread = dot_nt(
        jnp.where(iota((slots, experts), 1) == owner, 1.0, 0.0).astype(BF), table.astype(BF)
    )
    here = iota((slots, pair), 1) == iota((slots, pair), 0) % pair
    return jnp.sum(jnp.where(here, spread, 0.0), axis=1, keepdims=True)


def slot_row(table, core, slots):
    pair, experts = table.shape
    owner = 2 * (iota((experts, slots), 1) // pair) + core
    chosen = jnp.where(iota((experts, slots), 0) == owner, 1.0, 0.0).astype(BF)
    spread = dot(table.astype(BF), chosen)
    here = iota((pair, slots), 0) == iota((pair, slots), 1) % pair
    return jnp.sum(jnp.where(here, spread, 0.0), axis=0, keepdims=True)


def row_picker(slot_ref, ids, slots, count):
    token = slot_column(slot_ref[...].astype(F32), ids[0], slots)
    picker = jnp.where(iota((slots, count), 1).astype(F32) == token, 1.0, 0.0).astype(BF)
    return token, picker


def started(source, target, sem):
    copy = pltpu.make_async_copy(source, target, sem)
    copy.start()
    return copy


def leave_blocks(blocks, buffer, out_ref, sems):
    width = buffer.shape[1] // len(blocks)
    copies = []
    for n, half in enumerate(blocks):
        at = pl.ds(n * width, width)
        buffer[:, at] = half()
        copies.append(started(buffer.at[:, at], out_ref.at[:, at], sems.at[n]))
    for copy in copies:
        copy.wait()


def pick_own(ids, slot_hbm, tokens_hbm, half_ref, picker_ref, slot_ref, tokens_ref, sems):
    slots = half_ref.shape[0]
    slot_in = started(slot_hbm, slot_ref, sems.at[0])
    tokens_in = started(tokens_hbm, tokens_ref, sems.at[1])
    slot_in.wait()
    token, picker = row_picker(slot_ref, ids, slots, tokens_ref.shape[0])
    picker_ref[...] = picker
    tokens_in.wait()
    half_ref[...] = jnp.where(token < 0.0, EMPTY_MARK, dot(picker, tokens_ref[...])).astype(BF)


def pick_other(ids, half_ref, picker_ref, tokens_ref, sent_hbm, buffer, sems):
    slots, width = half_ref.shape
    stores = [started(half_ref, sent_hbm.at[:, pl.ds(0, width)], sems.at[0])]
    chunk = slots // 2
    for n in range(2):
        at = pl.ds(n * chunk, chunk)
        picker = picker_ref[at, :]
        empty = jnp.sum(picker.astype(F32), axis=1, keepdims=True) < 0.5
        buffer[at, :] = jnp.where(empty, EMPTY_MARK, dot(picker, tokens_ref[...])).astype(BF)
        stores.append(
            started(buffer.at[at, :], sent_hbm.at[at, pl.ds(width, width)], sems.at[1 + n])
        )
    for store in stores:
        store.wait()


def pick_grads(ids, slot_ref, gate_ref, own_ref, other_ref, sent_ref, buffer, sems):
    slots, both = sent_ref.shape
    token, picker = row_picker(slot_ref, ids, slots, own_ref.shape[0])
    gate = slot_column(gate_ref[...].astype(F32), ids[0], slots)
    leave_blocks(
        [
            lambda ref=ref: (gate * dot(picker, ref[...])).astype(BF)
            for ref in (own_ref, other_ref)
        ],
        buffer, sent_ref, sems,
    )


def send_chunks(ids, total_ref, own_ref, send_refs):
    chunk = own_ref.shape[0]
    parts = total_ref.shape[0] // chunk
    for k, ref in enumerate((own_ref, *send_refs)):
        at = pl.multiple_of(((ids[1] + k) % parts) * chunk, chunk)
        ref[...] = total_ref[pl.ds(at, chunk), :].astype(ref.dtype)


def join_chunks(ids, refs, whole_ref):
    chunk = refs[0].shape[0]
    parts = whole_ref.shape[0] // chunk
    for k, ref in enumerate(refs):
        at = pl.multiple_of(((ids[1] + parts - k) % parts) * chunk, chunk)
        whole_ref[pl.ds(at, chunk), :] = ref[...]


def forward_in(ids, got_hbm, wo_u_hbm, wg_ref, wu_ref, wo_g_ref,
               rows_hbm, narrow_hbm, widen_ref, own_ref, s1, s2, s3,
               total_ref, got_ref, rows_ref, narrow_ref, wo_u_ref, before_ref, sems):
    slots, both = got_ref.shape
    width, hidden = wg_ref.shape
    live_rows = rows_ref.shape[0]
    first, rest = pl.ds(0, 128), pl.ds(128, both - 128)
    first_in = started(got_hbm.at[:, first], got_ref.at[:, first], sems.at[0])
    rest_in = started(got_hbm.at[:, rest], got_ref.at[:, rest], sems.at[1])
    wo_u_in = started(wo_u_hbm, wo_u_ref, sems.at[4])
    before = iota((slots, slots), 0) <= iota((slots, slots), 1)
    before_ref[...] = jnp.where(before, 1.0, 0.0).astype(BF)
    lane0 = jnp.where(iota((8, 128), 1) == 0, 1.0, 0.0).astype(BF)
    first_in.wait()
    live_row = dot_nt(lane0, got_ref[:, :128]) < EMPTY_MARK / 2
    place_row = dot(jnp.where(live_row, 1.0, 0.0).astype(BF), before_ref[...])
    place_row = jnp.where(live_row, place_row - 1.0, -1.0)[:1, :]
    narrow = jnp.where(iota((live_rows, slots), 0).astype(F32) == place_row, 1.0, 0.0).astype(BF)
    narrow_ref[...] = narrow
    narrow_out = started(narrow_ref, narrow_hbm, sems.at[2])
    widen_ref[...] = narrow_ref[...].T
    rest_in.wait()
    rows_ref[...] = dot(narrow, got_ref[...]).astype(BF)
    rows_out = started(rows_ref, rows_hbm, sems.at[3])
    mine = rows_ref[:, :width]
    other = rows_ref[:, width:]
    total_ref[:, :hidden] = dot(mine, wg_ref[...]) + dot(other, wo_g_ref[...])
    wo_u_in.wait()
    total_ref[:, hidden:] = dot(mine, wu_ref[...]) + dot(other, wo_u_ref[...])
    send_chunks(ids, total_ref, own_ref, (s1, s2, s3))
    narrow_out.wait()
    rows_out.wait()


def activate(ids, own_ref, r1, r2, r3, pre_ref, hidden_ref):
    hidden = hidden_ref.shape[1]
    pre = own_ref[...] + r1[...].astype(F32) + r2[...].astype(F32) + r3[...].astype(F32)
    pre_ref[...] = pre
    hidden_ref[...] = (jax.nn.silu(pre[:, :hidden]) * pre[:, hidden:]).astype(BF)


def forward_out(ids, h0, h1, h2, h3, wd_ref, wo_d_ref, widen_ref, pre_ref, hidden_hbm, sent_ref,
                widen_hbm, pre_hbm, buffer, sems, hidden_ref, more_sems):
    kept = [
        started(widen_ref, widen_hbm, more_sems.at[0]),
        started(pre_ref, pre_hbm, more_sems.at[1]),
    ]
    join_chunks(ids, (h0, h1, h2, h3), hidden_ref)
    kept.append(started(hidden_ref, hidden_hbm, more_sems.at[2]))
    half = wd_ref.shape[1] // 2
    leave_blocks(
        [
            lambda ref=ref, at=at: dot(
                widen_ref[...], dot(hidden_ref[...], ref[:, at : at + half]).astype(BF)
            ).astype(BF)
            for ref in (wd_ref, wo_d_ref)
            for at in (0, half)
        ],
        buffer, sent_ref, sems,
    )
    for copy in kept:
        copy.wait()


def backward_in(ids, got_hbm, narrow_hbm, wd_hbm, wo_d_hbm, rows_hbm, own_ref, s1, s2, s3,
                total_ref, got_ref, narrow_ref, wd_ref, wo_d_ref, rows_ref, sems):
    width = wd_ref.shape[1]
    narrow_in = started(narrow_hbm, narrow_ref, sems.at[0])
    mine, other = pl.ds(0, width), pl.ds(width, width)
    mine_in = started(got_hbm.at[:, mine], got_ref.at[:, mine], sems.at[1])
    other_in = started(got_hbm.at[:, other], got_ref.at[:, other], sems.at[2])
    wd_in = started(wd_hbm, wd_ref, sems.at[3])
    wo_d_in = started(wo_d_hbm, wo_d_ref, sems.at[4])
    narrow_in.wait()
    mine_in.wait()
    rows_ref[:, :width] = dot(narrow_ref[...], got_ref[:, :width]).astype(BF)
    other_in.wait()
    rows_ref[:, width:] = dot(narrow_ref[...], got_ref[:, width:]).astype(BF)
    rows_out = started(rows_ref, rows_hbm, sems.at[5])
    wd_in.wait()
    total_ref[...] = dot_nt(rows_ref[:, :width], wd_ref[...])
    wo_d_in.wait()
    total_ref[...] += dot_nt(rows_ref[:, width:], wo_d_ref[...])
    send_chunks(ids, total_ref, own_ref, (s1, s2, s3))
    rows_out.wait()


def deactivate(ids, own_ref, r1, r2, r3, pre_ref, out_ref):
    hidden = own_ref.shape[1]
    grad = own_ref[...] + r1[...].astype(F32) + r2[...].astype(F32) + r3[...].astype(F32)
    gate_pre = pre_ref[:, :hidden]
    up_pre = pre_ref[:, hidden:]
    sigma = jax.nn.sigmoid(gate_pre)
    slope = sigma * (1.0 + gate_pre * (1.0 - sigma))
    out_ref[:, :hidden] = (grad * up_pre * slope).astype(BF)
    out_ref[:, hidden:] = (grad * (gate_pre * sigma)).astype(BF)


def backward_out(ids, g0, g1, g2, g3, wg_ref, wu_ref, wo_g_ref, wo_u_ref, widen_ref,
                 grads_hbm, sent_ref, buffer, sems, grads_ref, grads_sems):
    join_chunks(ids, (g0, g1, g2, g3), grads_ref)
    grads_out = started(grads_ref, grads_hbm, grads_sems.at[0])
    hidden = wg_ref.shape[1]
    gate = grads_ref[:, :hidden]
    up = grads_ref[:, hidden:]
    widen = widen_ref[...]

    def half(gate_w, up_w):
        back = dot_nt(gate, gate_w[...]) + dot_nt(up, up_w[...])
        return dot(widen, back.astype(BF)).astype(BF)

    leave_blocks(
        [lambda: half(wg_ref, wu_ref), lambda: half(wo_g_ref, wo_u_ref)], buffer, sent_ref, sems
    )
    grads_out.wait()


def fetch(ids, source_hbm, out_ref, sems):
    started(source_hbm, out_ref, sems.at[0]).wait()


def combine_out(ids, back_hbm, own_hbm, other_hbm, slot_ref, gate_ref, mine_hbm, theirs_ref,
                dots_ref, back_ref, own_ref, other_ref, mine_ref, sems):
    slots, both = back_ref.shape
    count, width = own_ref.shape
    pair = slot_ref.shape[0]
    mine, other = pl.ds(0, width), pl.ds(width, width)
    back_mine = started(back_hbm.at[:, mine], back_ref.at[:, mine], sems.at[0])
    own_in = started(own_hbm, own_ref, sems.at[1])
    back_other = started(back_hbm.at[:, other], back_ref.at[:, other], sems.at[2])
    other_in = started(other_hbm, other_ref, sems.at[3])
    token_row = slot_row(slot_ref[...].astype(F32), ids[0], slots)
    gate_row = slot_row(gate_ref[...].astype(F32), ids[0], slots)
    adder = jnp.where(
        iota((count, slots), 0).astype(F32) == token_row, gate_row, 0.0
    ).astype(BF)
    token, picker = row_picker(slot_ref, ids, slots, count)
    back_mine.wait()
    mine_ref[...] = dot(adder, back_ref[:, :width])
    mine_out = started(mine_ref, mine_hbm, sems.at[4])
    own_in.wait()
    sums = jnp.sum(
        dot(picker, own_ref[...]) * back_ref[:, :width].astype(F32), axis=1, keepdims=True
    )
    back_other.wait()
    theirs_ref[...] = dot(adder, back_ref[:, width:])
    other_in.wait()
    sums = sums + jnp.sum(
        dot(picker, other_ref[...]) * back_ref[:, width:].astype(F32), axis=1, keepdims=True
    )
    here = iota((slots, pair), 1) == iota((slots, pair), 0) % pair
    spread = jnp.where(here, sums, 0.0)
    dots_ref[...] = jnp.sum(spread.reshape(slots // pair, pair, pair), axis=1)
    mine_out.wait()


def adder_of(ids, slot_ref, count, slots):
    token_row = slot_row(slot_ref[...].astype(F32), ids[0], slots)
    return jnp.where(iota((count, slots), 0).astype(F32) == token_row, 1.0, 0.0).astype(BF)


def combine_theirs(ids, back_ref, slot_ref, theirs_ref):
    count, width = theirs_ref.shape
    adder = adder_of(ids, slot_ref, count, back_ref.shape[0])
    theirs_ref[...] = dot(adder, back_ref[:, width:])


def combine_mine(ids, back_ref, slot_ref, mine_ref):
    count, width = mine_ref.shape
    adder = adder_of(ids, slot_ref, count, back_ref.shape[0])
    mine_ref[...] = dot(adder, back_ref[:, :width])


def load_rows(rows_in_hbm, grads_hbm, hidden_hbm, rows_grad_hbm, at, refs, sems):
    sources = (rows_in_hbm.at[:, at], grads_hbm, rows_grad_hbm.at[:, at], hidden_hbm)
    return [started(source, ref, sems.at[n]) for n, (source, ref) in enumerate(zip(sources, refs))]


def weights_theirs(ids, rows_in_hbm, grads_hbm, hidden_hbm, rows_grad_hbm, in_ref, down_ref,
                   rows_in_ref, grads_ref, rows_grad_ref, hidden_ref, sems):
    width = in_ref.shape[0]
    loads = load_rows(rows_in_hbm, grads_hbm, hidden_hbm, rows_grad_hbm, pl.ds(width, width),
                      (rows_in_ref, grads_ref, rows_grad_ref, hidden_ref), sems)
    loads[0].wait()
    loads[1].wait()
    in_ref[...] = dot_tn(rows_in_ref[...], grads_ref[...]).astype(BF)
    loads[2].wait()
    loads[3].wait()
    down_ref[...] = dot_tn(hidden_ref[...], rows_grad_ref[...]).astype(BF)


def weights_mine(ids, rows_in_hbm, grads_hbm, hidden_hbm, rows_grad_hbm, gate_ref, up_ref, down_ref,
                 rows_in_ref, grads_ref, rows_grad_ref, hidden_ref, mine_in, mine_down, sems):
    width, hidden = gate_ref.shape[1:]
    core = ids[0]
    loads = load_rows(rows_in_hbm, grads_hbm, hidden_hbm, rows_grad_hbm, pl.ds(0, width),
                      (rows_in_ref, grads_ref, rows_grad_ref, hidden_ref), sems)
    loads[0].wait()
    loads[1].wait()
    mine_in[...] = dot_tn(rows_in_ref[...], grads_ref[...]).astype(BF)
    stores = [
        started(mine_in.at[:, pl.ds(0, hidden)], gate_ref.at[core], sems.at[4]),
        started(mine_in.at[:, pl.ds(hidden, hidden)], up_ref.at[core], sems.at[5]),
    ]
    loads[2].wait()
    loads[3].wait()
    mine_down[...] = dot_tn(hidden_ref[...], rows_grad_ref[...]).astype(BF)
    stores.append(started(mine_down, down_ref.at[core], sems.at[6]))
    for store in stores:
        store.wait()


def weights_got(ids, got_in_ref, got_down_ref, gate_in, up_in, down_in, gate_ref, up_ref, down_ref,
                sems):
    hidden = gate_ref.shape[2]
    there = 1 - ids[0]
    stores = [
        started(got_in_ref.at[:, pl.ds(0, hidden)], gate_ref.at[there], sems.at[0]),
        started(got_in_ref.at[:, pl.ds(hidden, hidden)], up_ref.at[there], sems.at[1]),
        started(got_down_ref, down_ref.at[there], sems.at[2]),
    ]
    for store in stores:
        store.wait()


def local(tokens, out_grad, slot_token, slot_gate, w_gate, w_up, w_down):
    senders = lax.axis_size("expert")
    devices = lax.axis_size("dp")
    parts = devices // 2
    count, width = tokens.shape
    both = 2 * width
    experts, pair = slot_token.shape[1:]
    hidden = w_gate.shape[2]
    slots = senders * pair
    chunk = LIVE // parts
    place = lax.axis_index("dp")
    core = place % 2
    ids = jnp.stack([core, place // 2]).astype(jnp.int32)
    slot_table = slot_token[0].T
    gate_table = slot_gate[0].T

    def swap(value):
        return lax.ppermute(value, "dp", [(i, i ^ 1) for i in range(devices)])

    def along(value, k):
        return lax.ppermute(value, "dp", [(i, (i + 2 * k) % devices) for i in range(devices)])

    def spread(values):
        return [along(value, k + 1) for k, value in enumerate(values)]

    def gather_x(value):
        return [value] + spread([value] * (parts - 1))

    def exchange(value):
        value = value.reshape(senders, pair, both)
        value = lax.all_to_all(value, "expert", split_axis=0, concat_axis=0, tiled=True)
        return value.reshape(slots, both)

    def pick_expert(value, which):
        return lax.dynamic_index_in_dim(value, which, 0, keepdims=False)

    tok_other = swap(tokens)
    grad_other = swap(out_grad)
    wg, wu, wd = (pick_expert(w, core) for w in (w_gate, w_up, w_down))
    wo_g, wo_u, wo_d = (swap(pick_expert(w, 1 - core)) for w in (w_gate, w_up, w_down))
    picks = 4 * slots * count * width
    move = 4 * LIVE * slots * width
    mm = 4 * LIVE * width * hidden
    sent = ((slots, both), BF)
    buffers = [pltpu.VMEM((slots, both), BF), pltpu.SemaphoreType.DMA((4,))]

    def room(*shapes):
        return [pltpu.VMEM(shape, dtype) for shape, dtype in shapes]

    def sems(n):
        return [pltpu.SemaphoreType.DMA((n,))]

    own_half, picker = call(
        pick_own, ids, (slot_table, tokens), [((slots, width), BF), ((slots, count), BF)],
        picks // 2, room((slot_table.shape, jnp.int32), (tokens.shape, BF)) + sems(2), (), (0, 1),
    )
    (sent_in,) = call(
        pick_other, ids, (own_half, picker, tok_other), [sent], picks // 2,
        room(((slots, width), BF)) + sems(3), (0,),
    )
    got_in = exchange(sent_in)
    (sent_grad,) = call(
        pick_grads, ids, (slot_table, gate_table, out_grad, grad_other), [sent], picks, buffers, (0,)
    )
    sent_grad, wg, wu, wd, wo_g, wo_u, wo_d = lax.optimization_barrier(
        (sent_grad, wg, wu, wd, wo_g, wo_u, wo_d)
    )
    got_grad = exchange(sent_grad)

    rows_in, narrow, widen, own, *sends = call(
        forward_in,
        ids,
        (got_in, wo_u, wg, wu, wo_g),
        [
            ((LIVE, both), BF),
            ((LIVE, slots), BF),
            ((slots, LIVE), BF),
            ((chunk, 2 * hidden), F32),
        ]
        + [((chunk, 2 * hidden), BF)] * (parts - 1),
        move + 2 * mm,
        room(
            ((LIVE, 2 * hidden), F32),
            ((slots, both), BF),
            ((LIVE, both), BF),
            ((LIVE, slots), BF),
            ((width, hidden), BF),
            ((slots, slots), BF),
        )
        + sems(5),
        (0, 1),
        (0, 1),
    )
    pre, hidden_own = call(
        activate,
        ids,
        (own, *spread(sends)),
        [((chunk, 2 * hidden), F32), ((chunk, hidden), BF)],
        8 * chunk * hidden,
    )
    hidden_all, sent_out, widen, pre = call(
        forward_out,
        ids,
        (*gather_x(hidden_own), wd, wo_d, widen, pre),
        [((LIVE, hidden), BF), sent, ((slots, LIVE), BF), ((chunk, 2 * hidden), F32)],
        move + mm,
        buffers + room(((LIVE, hidden), BF)) + sems(3),
        (0, 1, 2, 3),
    )
    back_out = exchange(sent_out)

    rows_grad, own, *sends = call(
        backward_in,
        ids,
        (got_grad, narrow, wd, wo_d),
        [((LIVE, both), BF), ((chunk, hidden), F32)] + [((chunk, hidden), BF)] * (parts - 1),
        move + mm,
        room(
            ((LIVE, hidden), F32),
            ((slots, both), BF),
            ((LIVE, slots), BF),
            ((hidden, width), BF),
            ((hidden, width), BF),
            ((LIVE, both), BF),
        )
        + sems(6),
        (0,),
        (0, 1, 2, 3),
    )
    (pre_grads,) = call(
        deactivate,
        ids,
        (own, *spread(sends), pre),
        [((chunk, 2 * hidden), BF)],
        12 * chunk * hidden,
    )
    wo_u, pre_grads = lax.optimization_barrier((wo_u, pre_grads))
    (wo_u,) = call(fetch, ids, (wo_u,), [(wo_u.shape, BF)], 0, sems(1), (), (0,))
    grads_all, sent_back = call(
        backward_out,
        ids,
        (*gather_x(pre_grads), wg, wu, wo_g, wo_u, widen),
        [((LIVE, 2 * hidden), BF), sent],
        move + 2 * mm,
        buffers + room(((LIVE, 2 * hidden), BF)) + sems(1),
        (0, 1),
    )
    back_grad = exchange(sent_back)

    out_mine, out_theirs, dots = call(
        combine_out,
        ids,
        (back_out, out_grad, grad_other, slot_table, gate_table),
        [((count, width), F32), ((count, width), F32), ((senders, pair), F32)],
        2 * picks,
        room(
            ((slots, both), BF), ((count, width), BF), ((count, width), BF), ((count, width), F32)
        )
        + sems(5),
        (0,),
        (0, 1, 2),
    )
    rows_in, grads_all, hidden_all, rows_grad, out_theirs, dots = lax.optimization_barrier(
        (rows_in, grads_all, hidden_all, rows_grad, out_theirs, dots)
    )
    rows = (rows_in, grads_all, hidden_all, rows_grad)
    rows_room = room(
        ((LIVE, width), BF), ((LIVE, 2 * hidden), BF), ((LIVE, width), BF), ((LIVE, hidden), BF)
    )
    theirs_in, theirs_down = call(
        weights_theirs,
        ids,
        rows,
        [((width, 2 * hidden), BF), ((hidden, width), BF)],
        3 * mm // 2,
        rows_room + sems(4),
        (),
        (0, 1, 2, 3),
    )
    weight_shapes = [(w_gate.shape, BF), (w_up.shape, BF), (w_down.shape, BF)]
    weight_grads = call(
        weights_mine,
        ids,
        rows,
        weight_shapes,
        3 * mm // 2,
        rows_room + room(((width, 2 * hidden), BF), ((hidden, width), BF)) + sems(7),
        (0, 1, 2),
        (0, 1, 2, 3),
    )
    moe_out = (out_mine + swap(out_theirs)).astype(BF)
    *dots, weight_grads = lax.optimization_barrier((*gather_x(dots), weight_grads))
    dots = sum(dots).astype(BF)
    dots_other = swap(dots)
    gate_grad = jnp.where(
        core == 0, jnp.stack([dots, dots_other], 1), jnp.stack([dots_other, dots], 1)
    )
    gate_grad = gate_grad.reshape(experts, pair).T
    grad_gate_w, grad_up_w, grad_down_w = call(
        weights_got,
        ids,
        (swap(theirs_in), swap(theirs_down), *weight_grads),
        weight_shapes,
        0,
        sems(3),
        (0, 1, 2),
        (2, 3, 4),
        ((2, 0), (3, 1), (4, 2)),
    )
    back_grad, moe_out, gate_grad, grad_gate_w, grad_up_w, grad_down_w = lax.optimization_barrier(
        (back_grad, moe_out, gate_grad, grad_gate_w, grad_up_w, grad_down_w)
    )
    half = [((count, width), F32)]
    (tok_theirs,) = call(combine_theirs, ids, (back_grad, slot_table), half, picks // 2)
    (tok_mine,) = call(combine_mine, ids, (back_grad, slot_table), half, picks // 2)
    token_grad = (tok_mine + swap(tok_theirs)).astype(BF)
    gate_grad = gate_grad.T.reshape(1, experts, pair)
    return (moe_out, token_grad, gate_grad, grad_gate_w, grad_up_w, grad_down_w)


def solution(mesh):
    placed = (
        P("expert", "dp"),
        P("expert", "dp"),
        P("expert", None, None),
        P("expert", None, None),
        P("expert", "dp", None),
        P("expert", "dp", None),
        P("expert", None, "dp"),
    )
    return jax.shard_map(
        local,
        mesh=mesh,
        in_specs=placed,
        out_specs=(
            P("expert", "dp"),
            P("expert", "dp"),
            P("expert", None, None),
            P("expert", "dp", None),
            P("expert", "dp", None),
            P("expert", None, "dp"),
        ),
        check_vma=False,
    )
```

```python
import functools

import jax
import jax.numpy as jnp
from jax import lax
from jax.experimental import pallas as pl
from jax.experimental.pallas import tpu as pltpu
from jax.sharding import PartitionSpec as P

BF = jnp.bfloat16
F32 = jnp.float32
LIVE = 256
EMPTY_MARK = 64.0
VMEM_LIMIT = 24 * 1024 * 1024


def dot(a, b):
    return jnp.dot(a, b, preferred_element_type=F32)


def dot_nt(a, b):
    return lax.dot_general(a, b, (((1,), (1,)), ((), ())), preferred_element_type=F32)


def dot_tn(a, b):
    return lax.dot_general(a, b, (((0,), (0,)), ((), ())), preferred_element_type=F32)


def iota(shape, dim):
    return lax.broadcasted_iota(jnp.int32, shape, dim)


IN_VMEM = pl.BlockSpec(memory_space=pltpu.VMEM)
IN_HBM = pl.BlockSpec(memory_space=pltpu.HBM)


def call(kernel, ids, args, outs, flops, scratch=(), placed=(), left=(), aliases=()):
    moved = sum(a.size * a.dtype.itemsize for a in args)
    moved += sum(functools.reduce(lambda p, q: p * q, s) * jnp.dtype(t).itemsize for s, t in outs)
    args = [
        pltpu.with_memory_space_constraint(a, pltpu.HBM) if n in left else a
        for n, a in enumerate(args)
    ]
    return pl.pallas_call(
        kernel,
        out_shape=[
            pltpu.HBM(s, t) if n in placed else jax.ShapeDtypeStruct(s, t)
            for n, (s, t) in enumerate(outs)
        ],
        in_specs=[pl.BlockSpec(memory_space=pltpu.SMEM)]
        + [IN_HBM if n in left else IN_VMEM for n in range(len(args))],
        out_specs=[IN_HBM if n in placed else IN_VMEM for n in range(len(outs))],
        scratch_shapes=list(scratch),
        input_output_aliases={n + 1: m for n, m in aliases},
        cost_estimate=pl.CostEstimate(flops=flops, bytes_accessed=moved, transcendentals=0),
        compiler_params=pltpu.CompilerParams(vmem_limit_bytes=VMEM_LIMIT),
    )(ids, *args)


def slot_column(table, core, slots):
    pair, experts = table.shape
    owner = 2 * (iota((slots, experts), 0) // pair) + core
    spread = dot_nt(
        jnp.where(iota((slots, experts), 1) == owner, 1.0, 0.0).astype(BF), table.astype(BF)
    )
    here = iota((slots, pair), 1) == iota((slots, pair), 0) % pair
    return jnp.sum(jnp.where(here, spread, 0.0), axis=1, keepdims=True)


def slot_row(table, core, slots):
    pair, experts = table.shape
    owner = 2 * (iota((experts, slots), 1) // pair) + core
    chosen = jnp.where(iota((experts, slots), 0) == owner, 1.0, 0.0).astype(BF)
    spread = dot(table.astype(BF), chosen)
    here = iota((pair, slots), 0) == iota((pair, slots), 1) % pair
    return jnp.sum(jnp.where(here, spread, 0.0), axis=0, keepdims=True)


def row_picker(slot_ref, ids, slots, count):
    token = slot_column(slot_ref[...].astype(F32), ids[0], slots)
    picker = jnp.where(iota((slots, count), 1).astype(F32) == token, 1.0, 0.0).astype(BF)
    return token, picker


def started(source, target, sem):
    copy = pltpu.make_async_copy(source, target, sem)
    copy.start()
    return copy


def leave_blocks(blocks, buffer, out_ref, sems):
    width = buffer.shape[1] // len(blocks)
    copies = []
    for n, half in enumerate(blocks):
        at = pl.ds(n * width, width)
        buffer[:, at] = half()
        copies.append(started(buffer.at[:, at], out_ref.at[:, at], sems.at[n]))
    for copy in copies:
        copy.wait()


def pick_own(ids, slot_hbm, tokens_hbm, half_ref, picker_ref, slot_ref, tokens_ref, sems):
    slots = half_ref.shape[0]
    slot_in = started(slot_hbm, slot_ref, sems.at[0])
    tokens_in = started(tokens_hbm, tokens_ref, sems.at[1])
    slot_in.wait()
    token, picker = row_picker(slot_ref, ids, slots, tokens_ref.shape[0])
    picker_ref[...] = picker
    tokens_in.wait()
    half_ref[...] = jnp.where(token < 0.0, EMPTY_MARK, dot(picker, tokens_ref[...])).astype(BF)


def pick_other(ids, half_ref, picker_ref, tokens_ref, sent_hbm, buffer, sems):
    slots, width = half_ref.shape
    stores = [started(half_ref, sent_hbm.at[:, pl.ds(0, width)], sems.at[0])]
    chunk = slots // 2
    for n in range(2):
        at = pl.ds(n * chunk, chunk)
        picker = picker_ref[at, :]
        empty = jnp.sum(picker.astype(F32), axis=1, keepdims=True) < 0.5
        buffer[at, :] = jnp.where(empty, EMPTY_MARK, dot(picker, tokens_ref[...])).astype(BF)
        stores.append(
            started(buffer.at[at, :], sent_hbm.at[at, pl.ds(width, width)], sems.at[1 + n])
        )
    for store in stores:
        store.wait()


def pick_grads(ids, slot_ref, gate_ref, own_ref, other_ref, sent_ref, buffer, sems):
    slots, both = sent_ref.shape
    token, picker = row_picker(slot_ref, ids, slots, own_ref.shape[0])
    gate = slot_column(gate_ref[...].astype(F32), ids[0], slots)
    leave_blocks(
        [
            lambda ref=ref: (gate * dot(picker, ref[...])).astype(BF)
            for ref in (own_ref, other_ref)
        ],
        buffer, sent_ref, sems,
    )


def send_chunks(ids, total_ref, own_ref, send_refs):
    chunk = own_ref.shape[0]
    parts = total_ref.shape[0] // chunk
    for k, ref in enumerate((own_ref, *send_refs)):
        at = pl.multiple_of(((ids[1] + k) % parts) * chunk, chunk)
        ref[...] = total_ref[pl.ds(at, chunk), :].astype(ref.dtype)


def join_chunks(ids, refs, whole_ref):
    chunk = refs[0].shape[0]
    parts = whole_ref.shape[0] // chunk
    for k, ref in enumerate(refs):
        at = pl.multiple_of(((ids[1] + parts - k) % parts) * chunk, chunk)
        whole_ref[pl.ds(at, chunk), :] = ref[...]


def forward_in(ids, got_hbm, wo_u_hbm, wg_ref, wu_ref, wo_g_ref,
               rows_hbm, narrow_hbm, widen_ref, own_ref, s1, s2, s3,
               total_ref, got_ref, rows_ref, narrow_ref, wo_u_ref, before_ref, sems):
    slots, both = got_ref.shape
    width, hidden = wg_ref.shape
    live_rows = rows_ref.shape[0]
    first, rest = pl.ds(0, 128), pl.ds(128, both - 128)
    first_in = started(got_hbm.at[:, first], got_ref.at[:, first], sems.at[0])
    rest_in = started(got_hbm.at[:, rest], got_ref.at[:, rest], sems.at[1])
    wo_u_in = started(wo_u_hbm, wo_u_ref, sems.at[4])
    before = iota((slots, slots), 0) <= iota((slots, slots), 1)
    before_ref[...] = jnp.where(before, 1.0, 0.0).astype(BF)
    lane0 = jnp.where(iota((8, 128), 1) == 0, 1.0, 0.0).astype(BF)
    first_in.wait()
    live_row = dot_nt(lane0, got_ref[:, :128]) < EMPTY_MARK / 2
    place_row = dot(jnp.where(live_row, 1.0, 0.0).astype(BF), before_ref[...])
    place_row = jnp.where(live_row, place_row - 1.0, -1.0)[:1, :]
    narrow = jnp.where(iota((live_rows, slots), 0).astype(F32) == place_row, 1.0, 0.0).astype(BF)
    narrow_ref[...] = narrow
    narrow_out = started(narrow_ref, narrow_hbm, sems.at[2])
    widen_ref[...] = narrow_ref[...].T
    rest_in.wait()
    rows_ref[...] = dot(narrow, got_ref[...]).astype(BF)
    rows_out = started(rows_ref, rows_hbm, sems.at[3])
    mine = rows_ref[:, :width]
    other = rows_ref[:, width:]
    total_ref[:, :hidden] = dot(mine, wg_ref[...]) + dot(other, wo_g_ref[...])
    wo_u_in.wait()
    total_ref[:, hidden:] = dot(mine, wu_ref[...]) + dot(other, wo_u_ref[...])
    send_chunks(ids, total_ref, own_ref, (s1, s2, s3))
    narrow_out.wait()
    rows_out.wait()


def activate(ids, own_ref, r1, r2, r3, pre_ref, hidden_ref):
    hidden = hidden_ref.shape[1]
    pre = own_ref[...] + r1[...].astype(F32) + r2[...].astype(F32) + r3[...].astype(F32)
    pre_ref[...] = pre
    hidden_ref[...] = (jax.nn.silu(pre[:, :hidden]) * pre[:, hidden:]).astype(BF)


def forward_out(ids, h0, h1, h2, h3, wd_ref, wo_d_ref, widen_ref, pre_ref, hidden_hbm, sent_ref,
                widen_hbm, pre_hbm, buffer, sems, hidden_ref, more_sems):
    kept = [
        started(widen_ref, widen_hbm, more_sems.at[0]),
        started(pre_ref, pre_hbm, more_sems.at[1]),
    ]
    join_chunks(ids, (h0, h1, h2, h3), hidden_ref)
    kept.append(started(hidden_ref, hidden_hbm, more_sems.at[2]))
    half = wd_ref.shape[1] // 2
    leave_blocks(
        [
            lambda out=out, at=at: dot(widen_ref[...], out[:, at : at + half]).astype(BF)
            for out in (
                dot(hidden_ref[...], wd_ref[...]).astype(BF),
                dot(hidden_ref[...], wo_d_ref[...]).astype(BF),
            )
            for at in (0, half)
        ],
        buffer, sent_ref, sems,
    )
    for copy in kept:
        copy.wait()


def backward_in(ids, got_hbm, narrow_hbm, wd_hbm, wo_d_hbm, rows_hbm, own_ref, s1, s2, s3,
                total_ref, got_ref, narrow_ref, wd_ref, wo_d_ref, rows_ref, sems):
    width = wd_ref.shape[1]
    narrow_in = started(narrow_hbm, narrow_ref, sems.at[0])
    mine, other = pl.ds(0, width), pl.ds(width, width)
    mine_in = started(got_hbm.at[:, mine], got_ref.at[:, mine], sems.at[1])
    other_in = started(got_hbm.at[:, other], got_ref.at[:, other], sems.at[2])
    wd_in = started(wd_hbm, wd_ref, sems.at[3])
    wo_d_in = started(wo_d_hbm, wo_d_ref, sems.at[4])
    narrow_in.wait()
    mine_in.wait()
    rows_ref[:, :width] = dot(narrow_ref[...], got_ref[:, :width]).astype(BF)
    other_in.wait()
    rows_ref[:, width:] = dot(narrow_ref[...], got_ref[:, width:]).astype(BF)
    rows_out = started(rows_ref, rows_hbm, sems.at[5])
    wd_in.wait()
    total_ref[...] = dot_nt(rows_ref[:, :width], wd_ref[...])
    wo_d_in.wait()
    total_ref[...] += dot_nt(rows_ref[:, width:], wo_d_ref[...])
    send_chunks(ids, total_ref, own_ref, (s1, s2, s3))
    rows_out.wait()


def deactivate(ids, own_ref, r1, r2, r3, pre_ref, out_ref):
    hidden = own_ref.shape[1]
    grad = own_ref[...] + r1[...].astype(F32) + r2[...].astype(F32) + r3[...].astype(F32)
    gate_pre = pre_ref[:, :hidden]
    up_pre = pre_ref[:, hidden:]
    sigma = jax.nn.sigmoid(gate_pre)
    slope = sigma * (1.0 + gate_pre * (1.0 - sigma))
    out_ref[:, :hidden] = (grad * up_pre * slope).astype(BF)
    out_ref[:, hidden:] = (grad * (gate_pre * sigma)).astype(BF)


def backward_out(ids, g0, g1, g2, g3, wg_ref, wu_ref, wo_g_ref, wo_u_ref, widen_ref,
                 grads_hbm, sent_ref, buffer, sems, grads_ref, grads_sems):
    join_chunks(ids, (g0, g1, g2, g3), grads_ref)
    grads_out = started(grads_ref, grads_hbm, grads_sems.at[0])
    hidden = wg_ref.shape[1]
    gate = grads_ref[:, :hidden]
    up = grads_ref[:, hidden:]
    widen = widen_ref[...]

    def half(gate_w, up_w):
        back = dot_nt(gate, gate_w[...]) + dot_nt(up, up_w[...])
        return dot(widen, back.astype(BF)).astype(BF)

    leave_blocks(
        [lambda: half(wg_ref, wu_ref), lambda: half(wo_g_ref, wo_u_ref)], buffer, sent_ref, sems
    )
    grads_out.wait()


def fetch(ids, source_hbm, out_ref, sems):
    started(source_hbm, out_ref, sems.at[0]).wait()


def combine_out(ids, back_hbm, own_hbm, other_hbm, slot_ref, gate_ref, mine_hbm, theirs_ref,
                dots_ref, back_ref, own_ref, other_ref, mine_ref, sems):
    slots, both = back_ref.shape
    count, width = own_ref.shape
    pair = slot_ref.shape[0]
    mine, other = pl.ds(0, width), pl.ds(width, width)
    back_mine = started(back_hbm.at[:, mine], back_ref.at[:, mine], sems.at[0])
    own_in = started(own_hbm, own_ref, sems.at[1])
    back_other = started(back_hbm.at[:, other], back_ref.at[:, other], sems.at[2])
    other_in = started(other_hbm, other_ref, sems.at[3])
    token_row = slot_row(slot_ref[...].astype(F32), ids[0], slots)
    gate_row = slot_row(gate_ref[...].astype(F32), ids[0], slots)
    adder = jnp.where(
        iota((count, slots), 0).astype(F32) == token_row, gate_row, 0.0
    ).astype(BF)
    token, picker = row_picker(slot_ref, ids, slots, count)
    back_mine.wait()
    mine_ref[...] = dot(adder, back_ref[:, :width])
    mine_out = started(mine_ref, mine_hbm, sems.at[4])
    own_in.wait()
    sums = jnp.sum(
        dot(picker, own_ref[...]) * back_ref[:, :width].astype(F32), axis=1, keepdims=True
    )
    back_other.wait()
    theirs_ref[...] = dot(adder, back_ref[:, width:])
    other_in.wait()
    sums = sums + jnp.sum(
        dot(picker, other_ref[...]) * back_ref[:, width:].astype(F32), axis=1, keepdims=True
    )
    here = iota((slots, pair), 1) == iota((slots, pair), 0) % pair
    spread = jnp.where(here, sums, 0.0)
    dots_ref[...] = jnp.sum(spread.reshape(slots // pair, pair, pair), axis=1)
    mine_out.wait()


def adder_of(ids, slot_ref, count, slots):
    token_row = slot_row(slot_ref[...].astype(F32), ids[0], slots)
    return jnp.where(iota((count, slots), 0).astype(F32) == token_row, 1.0, 0.0).astype(BF)


def combine_theirs(ids, back_ref, slot_ref, theirs_ref):
    count, width = theirs_ref.shape
    adder = adder_of(ids, slot_ref, count, back_ref.shape[0])
    theirs_ref[...] = dot(adder, back_ref[:, width:])


def combine_mine(ids, back_ref, slot_ref, mine_ref):
    count, width = mine_ref.shape
    adder = adder_of(ids, slot_ref, count, back_ref.shape[0])
    mine_ref[...] = dot(adder, back_ref[:, :width])


def load_rows(rows_in_hbm, grads_hbm, hidden_hbm, rows_grad_hbm, at, refs, sems):
    sources = (rows_in_hbm.at[:, at], grads_hbm, rows_grad_hbm.at[:, at], hidden_hbm)
    return [started(source, ref, sems.at[n]) for n, (source, ref) in enumerate(zip(sources, refs))]


def weights_theirs(ids, rows_in_hbm, grads_hbm, hidden_hbm, rows_grad_hbm, in_ref, down_ref,
                   rows_in_ref, grads_ref, rows_grad_ref, hidden_ref, sems):
    width = in_ref.shape[0]
    loads = load_rows(rows_in_hbm, grads_hbm, hidden_hbm, rows_grad_hbm, pl.ds(width, width),
                      (rows_in_ref, grads_ref, rows_grad_ref, hidden_ref), sems)
    loads[0].wait()
    loads[1].wait()
    in_ref[...] = dot_tn(rows_in_ref[...], grads_ref[...]).astype(BF)
    loads[2].wait()
    loads[3].wait()
    down_ref[...] = dot_tn(hidden_ref[...], rows_grad_ref[...]).astype(BF)


def weights_mine(ids, rows_in_hbm, grads_hbm, hidden_hbm, rows_grad_hbm, gate_ref, up_ref, down_ref,
                 rows_in_ref, grads_ref, rows_grad_ref, hidden_ref, mine_in, mine_down, sems):
    width, hidden = gate_ref.shape[1:]
    core = ids[0]
    loads = load_rows(rows_in_hbm, grads_hbm, hidden_hbm, rows_grad_hbm, pl.ds(0, width),
                      (rows_in_ref, grads_ref, rows_grad_ref, hidden_ref), sems)
    loads[0].wait()
    loads[1].wait()
    mine_in[...] = dot_tn(rows_in_ref[...], grads_ref[...]).astype(BF)
    stores = [
        started(mine_in.at[:, pl.ds(0, hidden)], gate_ref.at[core], sems.at[4]),
        started(mine_in.at[:, pl.ds(hidden, hidden)], up_ref.at[core], sems.at[5]),
    ]
    loads[2].wait()
    loads[3].wait()
    mine_down[...] = dot_tn(hidden_ref[...], rows_grad_ref[...]).astype(BF)
    stores.append(started(mine_down, down_ref.at[core], sems.at[6]))
    for store in stores:
        store.wait()


def weights_got(ids, got_in_ref, got_down_ref, gate_in, up_in, down_in, gate_ref, up_ref, down_ref,
                sems):
    hidden = gate_ref.shape[2]
    there = 1 - ids[0]
    stores = [
        started(got_in_ref.at[:, pl.ds(0, hidden)], gate_ref.at[there], sems.at[0]),
        started(got_in_ref.at[:, pl.ds(hidden, hidden)], up_ref.at[there], sems.at[1]),
        started(got_down_ref, down_ref.at[there], sems.at[2]),
    ]
    for store in stores:
        store.wait()


def local(tokens, out_grad, slot_token, slot_gate, w_gate, w_up, w_down):
    senders = lax.axis_size("expert")
    devices = lax.axis_size("dp")
    parts = devices // 2
    count, width = tokens.shape
    both = 2 * width
    experts, pair = slot_token.shape[1:]
    hidden = w_gate.shape[2]
    slots = senders * pair
    chunk = LIVE // parts
    place = lax.axis_index("dp")
    core = place % 2
    ids = jnp.stack([core, place // 2]).astype(jnp.int32)
    slot_table = slot_token[0].T
    gate_table = slot_gate[0].T

    def swap(value):
        return lax.ppermute(value, "dp", [(i, i ^ 1) for i in range(devices)])

    def along(value, k):
        return lax.ppermute(value, "dp", [(i, (i + 2 * k) % devices) for i in range(devices)])

    def spread(values):
        return [along(value, k + 1) for k, value in enumerate(values)]

    def gather_x(value):
        return [value] + spread([value] * (parts - 1))

    def exchange(value):
        value = value.reshape(senders, pair, both)
        value = lax.all_to_all(value, "expert", split_axis=0, concat_axis=0, tiled=True)
        return value.reshape(slots, both)

    def pick_expert(value, which):
        return lax.dynamic_index_in_dim(value, which, 0, keepdims=False)

    tok_other = swap(tokens)
    grad_other = swap(out_grad)
    wg, wu, wd = (pick_expert(w, core) for w in (w_gate, w_up, w_down))
    wo_g, wo_u, wo_d = (swap(pick_expert(w, 1 - core)) for w in (w_gate, w_up, w_down))
    picks = 4 * slots * count * width
    move = 4 * LIVE * slots * width
    mm = 4 * LIVE * width * hidden
    sent = ((slots, both), BF)
    buffers = [pltpu.VMEM((slots, both), BF), pltpu.SemaphoreType.DMA((4,))]

    def room(*shapes):
        return [pltpu.VMEM(shape, dtype) for shape, dtype in shapes]

    def sems(n):
        return [pltpu.SemaphoreType.DMA((n,))]

    own_half, picker = call(
        pick_own, ids, (slot_table, tokens), [((slots, width), BF), ((slots, count), BF)],
        picks // 2, room((slot_table.shape, jnp.int32), (tokens.shape, BF)) + sems(2), (), (0, 1),
    )
    (sent_in,) = call(
        pick_other, ids, (own_half, picker, tok_other), [sent], picks // 2,
        room(((slots, width), BF)) + sems(3), (0,),
    )
    got_in = exchange(sent_in)
    (sent_grad,) = call(
        pick_grads, ids, (slot_table, gate_table, out_grad, grad_other), [sent], picks, buffers, (0,)
    )
    sent_grad, wg, wu, wd, wo_g, wo_u, wo_d = lax.optimization_barrier(
        (sent_grad, wg, wu, wd, wo_g, wo_u, wo_d)
    )
    got_grad = exchange(sent_grad)

    rows_in, narrow, widen, own, *sends = call(
        forward_in,
        ids,
        (got_in, wo_u, wg, wu, wo_g),
        [
            ((LIVE, both), BF),
            ((LIVE, slots), BF),
            ((slots, LIVE), BF),
            ((chunk, 2 * hidden), F32),
        ]
        + [((chunk, 2 * hidden), BF)] * (parts - 1),
        move + 2 * mm,
        room(
            ((LIVE, 2 * hidden), F32),
            ((slots, both), BF),
            ((LIVE, both), BF),
            ((LIVE, slots), BF),
            ((width, hidden), BF),
            ((slots, slots), BF),
        )
        + sems(5),
        (0, 1),
        (0, 1),
    )
    pre, hidden_own = call(
        activate,
        ids,
        (own, *spread(sends)),
        [((chunk, 2 * hidden), F32), ((chunk, hidden), BF)],
        8 * chunk * hidden,
    )
    hidden_all, sent_out, widen, pre = call(
        forward_out,
        ids,
        (*gather_x(hidden_own), wd, wo_d, widen, pre),
        [((LIVE, hidden), BF), sent, ((slots, LIVE), BF), ((chunk, 2 * hidden), F32)],
        move + mm,
        buffers + room(((LIVE, hidden), BF)) + sems(3),
        (0, 1, 2, 3),
    )
    back_out = exchange(sent_out)

    rows_grad, own, *sends = call(
        backward_in,
        ids,
        (got_grad, narrow, wd, wo_d),
        [((LIVE, both), BF), ((chunk, hidden), F32)] + [((chunk, hidden), BF)] * (parts - 1),
        move + mm,
        room(
            ((LIVE, hidden), F32),
            ((slots, both), BF),
            ((LIVE, slots), BF),
            ((hidden, width), BF),
            ((hidden, width), BF),
            ((LIVE, both), BF),
        )
        + sems(6),
        (0,),
        (0, 1, 2, 3),
    )
    (pre_grads,) = call(
        deactivate,
        ids,
        (own, *spread(sends), pre),
        [((chunk, 2 * hidden), BF)],
        12 * chunk * hidden,
    )
    wo_u, pre_grads = lax.optimization_barrier((wo_u, pre_grads))
    (wo_u,) = call(fetch, ids, (wo_u,), [(wo_u.shape, BF)], 0, sems(1), (), (0,))
    grads_all, sent_back = call(
        backward_out,
        ids,
        (*gather_x(pre_grads), wg, wu, wo_g, wo_u, widen),
        [((LIVE, 2 * hidden), BF), sent],
        move + 2 * mm,
        buffers + room(((LIVE, 2 * hidden), BF)) + sems(1),
        (0, 1),
    )
    back_grad = exchange(sent_back)

    out_mine, out_theirs, dots = call(
        combine_out,
        ids,
        (back_out, out_grad, grad_other, slot_table, gate_table),
        [((count, width), F32), ((count, width), F32), ((senders, pair), F32)],
        2 * picks,
        room(
            ((slots, both), BF), ((count, width), BF), ((count, width), BF), ((count, width), F32)
        )
        + sems(5),
        (0,),
        (0, 1, 2),
    )
    rows_in, grads_all, hidden_all, rows_grad, out_theirs, dots = lax.optimization_barrier(
        (rows_in, grads_all, hidden_all, rows_grad, out_theirs, dots)
    )
    rows = (rows_in, grads_all, hidden_all, rows_grad)
    rows_room = room(
        ((LIVE, width), BF), ((LIVE, 2 * hidden), BF), ((LIVE, width), BF), ((LIVE, hidden), BF)
    )
    theirs_in, theirs_down = call(
        weights_theirs,
        ids,
        rows,
        [((width, 2 * hidden), BF), ((hidden, width), BF)],
        3 * mm // 2,
        rows_room + sems(4),
        (),
        (0, 1, 2, 3),
    )
    weight_shapes = [(w_gate.shape, BF), (w_up.shape, BF), (w_down.shape, BF)]
    weight_grads = call(
        weights_mine,
        ids,
        rows,
        weight_shapes,
        3 * mm // 2,
        rows_room + room(((width, 2 * hidden), BF), ((hidden, width), BF)) + sems(7),
        (0, 1, 2),
        (0, 1, 2, 3),
    )
    moe_out = (out_mine + swap(out_theirs)).astype(BF)
    *dots, weight_grads = lax.optimization_barrier((*gather_x(dots), weight_grads))
    dots = sum(dots).astype(BF)
    dots_other = swap(dots)
    gate_grad = jnp.where(
        core == 0, jnp.stack([dots, dots_other], 1), jnp.stack([dots_other, dots], 1)
    )
    gate_grad = gate_grad.reshape(experts, pair).T
    grad_gate_w, grad_up_w, grad_down_w = call(
        weights_got,
        ids,
        (swap(theirs_in), swap(theirs_down), *weight_grads),
        weight_shapes,
        0,
        sems(3),
        (0, 1, 2),
        (2, 3, 4),
        ((2, 0), (3, 1), (4, 2)),
    )
    back_grad, moe_out, gate_grad, grad_gate_w, grad_up_w, grad_down_w = lax.optimization_barrier(
        (back_grad, moe_out, gate_grad, grad_gate_w, grad_up_w, grad_down_w)
    )
    half = [((count, width), F32)]
    (tok_theirs,) = call(combine_theirs, ids, (back_grad, slot_table), half, picks // 2)
    (tok_mine,) = call(combine_mine, ids, (back_grad, slot_table), half, picks // 2)
    token_grad = (tok_mine + swap(tok_theirs)).astype(BF)
    gate_grad = gate_grad.T.reshape(1, experts, pair)
    return (moe_out, token_grad, gate_grad, grad_gate_w, grad_up_w, grad_down_w)


def solution(mesh):
    placed = (
        P("expert", "dp"),
        P("expert", "dp"),
        P("expert", None, None),
        P("expert", None, None),
        P("expert", "dp", None),
        P("expert", "dp", None),
        P("expert", None, "dp"),
    )
    return jax.shard_map(
        local,
        mesh=mesh,
        in_specs=placed,
        out_specs=(
            P("expert", "dp"),
            P("expert", "dp"),
            P("expert", None, None),
            P("expert", "dp", None),
            P("expert", "dp", None),
            P("expert", None, "dp"),
        ),
        check_vma=False,
    )
```

```python
import functools

import jax
import jax.numpy as jnp
from jax import lax
from jax.experimental import pallas as pl
from jax.experimental.pallas import tpu as pltpu
from jax.sharding import PartitionSpec as P

BF = jnp.bfloat16
F32 = jnp.float32
LIVE = 256
EMPTY_MARK = 64.0
VMEM_LIMIT = 24 * 1024 * 1024


def dot(a, b):
    return jnp.dot(a, b, preferred_element_type=F32)


def dot_nt(a, b):
    return lax.dot_general(a, b, (((1,), (1,)), ((), ())), preferred_element_type=F32)


def dot_tn(a, b):
    return lax.dot_general(a, b, (((0,), (0,)), ((), ())), preferred_element_type=F32)


def iota(shape, dim):
    return lax.broadcasted_iota(jnp.int32, shape, dim)


IN_VMEM = pl.BlockSpec(memory_space=pltpu.VMEM)
IN_HBM = pl.BlockSpec(memory_space=pltpu.HBM)


def call(kernel, ids, args, outs, flops, scratch=(), placed=(), left=(), aliases=()):
    moved = sum(a.size * a.dtype.itemsize for a in args)
    moved += sum(functools.reduce(lambda p, q: p * q, s) * jnp.dtype(t).itemsize for s, t in outs)
    args = [
        pltpu.with_memory_space_constraint(a, pltpu.HBM) if n in left else a
        for n, a in enumerate(args)
    ]
    return pl.pallas_call(
        kernel,
        out_shape=[
            pltpu.HBM(s, t) if n in placed else jax.ShapeDtypeStruct(s, t)
            for n, (s, t) in enumerate(outs)
        ],
        in_specs=[pl.BlockSpec(memory_space=pltpu.SMEM)]
        + [IN_HBM if n in left else IN_VMEM for n in range(len(args))],
        out_specs=[IN_HBM if n in placed else IN_VMEM for n in range(len(outs))],
        scratch_shapes=list(scratch),
        input_output_aliases={n + 1: m for n, m in aliases},
        cost_estimate=pl.CostEstimate(flops=flops, bytes_accessed=moved, transcendentals=0),
        compiler_params=pltpu.CompilerParams(vmem_limit_bytes=VMEM_LIMIT),
    )(ids, *args)


def slot_column(table, core, slots):
    pair, experts = table.shape
    owner = 2 * (iota((slots, experts), 0) // pair) + core
    spread = dot_nt(
        jnp.where(iota((slots, experts), 1) == owner, 1.0, 0.0).astype(BF), table.astype(BF)
    )
    here = iota((slots, pair), 1) == iota((slots, pair), 0) % pair
    return jnp.sum(jnp.where(here, spread, 0.0), axis=1, keepdims=True)


def slot_row(table, core, slots):
    pair, experts = table.shape
    owner = 2 * (iota((experts, slots), 1) // pair) + core
    chosen = jnp.where(iota((experts, slots), 0) == owner, 1.0, 0.0).astype(BF)
    spread = dot(table.astype(BF), chosen)
    here = iota((pair, slots), 0) == iota((pair, slots), 1) % pair
    return jnp.sum(jnp.where(here, spread, 0.0), axis=0, keepdims=True)


def row_picker(slot_ref, ids, slots, count):
    token = slot_column(slot_ref[...].astype(F32), ids[0], slots)
    picker = jnp.where(iota((slots, count), 1).astype(F32) == token, 1.0, 0.0).astype(BF)
    return token, picker


def started(source, target, sem):
    copy = pltpu.make_async_copy(source, target, sem)
    copy.start()
    return copy


def leave_blocks(blocks, buffer, out_ref, sems):
    width = buffer.shape[1] // len(blocks)
    copies = []
    for n, half in enumerate(blocks):
        at = pl.ds(n * width, width)
        buffer[:, at] = half()
        copies.append(started(buffer.at[:, at], out_ref.at[:, at], sems.at[n]))
    for copy in copies:
        copy.wait()


def pick_own(ids, slot_hbm, tokens_hbm, half_ref, picker_ref, slot_ref, tokens_ref, sems):
    slots = half_ref.shape[0]
    slot_in = started(slot_hbm, slot_ref, sems.at[0])
    tokens_in = started(tokens_hbm, tokens_ref, sems.at[1])
    slot_in.wait()
    token, picker = row_picker(slot_ref, ids, slots, tokens_ref.shape[0])
    picker_ref[...] = picker
    tokens_in.wait()
    half_ref[...] = jnp.where(token < 0.0, EMPTY_MARK, dot(picker, tokens_ref[...])).astype(BF)


def pick_other(ids, half_ref, picker_ref, tokens_ref, sent_hbm, buffer, sems):
    slots, width = half_ref.shape
    stores = [started(half_ref, sent_hbm.at[:, pl.ds(0, width)], sems.at[0])]
    chunk = slots // 2
    for n in range(2):
        at = pl.ds(n * chunk, chunk)
        picker = picker_ref[at, :]
        empty = jnp.sum(picker.astype(F32), axis=1, keepdims=True) < 0.5
        buffer[at, :] = jnp.where(empty, EMPTY_MARK, dot(picker, tokens_ref[...])).astype(BF)
        stores.append(
            started(buffer.at[at, :], sent_hbm.at[at, pl.ds(width, width)], sems.at[1 + n])
        )
    for store in stores:
        store.wait()


def pick_grads(ids, slot_ref, gate_ref, own_ref, other_ref, sent_ref, buffer, sems):
    slots, both = sent_ref.shape
    token, picker = row_picker(slot_ref, ids, slots, own_ref.shape[0])
    gate = slot_column(gate_ref[...].astype(F32), ids[0], slots)
    leave_blocks(
        [
            lambda ref=ref: (gate * dot(picker, ref[...])).astype(BF)
            for ref in (own_ref, other_ref)
        ],
        buffer, sent_ref, sems,
    )


def send_chunks(ids, total_ref, own_ref, send_refs):
    chunk = own_ref.shape[0]
    parts = total_ref.shape[0] // chunk
    for k, ref in enumerate((own_ref, *send_refs)):
        at = pl.multiple_of(((ids[1] + k) % parts) * chunk, chunk)
        ref[...] = total_ref[pl.ds(at, chunk), :].astype(ref.dtype)


def join_chunks(ids, refs, whole_ref):
    chunk = refs[0].shape[0]
    parts = whole_ref.shape[0] // chunk
    for k, ref in enumerate(refs):
        at = pl.multiple_of(((ids[1] + parts - k) % parts) * chunk, chunk)
        whole_ref[pl.ds(at, chunk), :] = ref[...]


def forward_in(ids, got_hbm, wo_u_hbm, wg_ref, wu_ref, wo_g_ref,
               rows_hbm, narrow_hbm, widen_ref, own_ref, s1, s2, s3,
               total_ref, got_ref, rows_ref, narrow_ref, wo_u_ref, before_ref, sems):
    slots, both = got_ref.shape
    width, hidden = wg_ref.shape
    live_rows = rows_ref.shape[0]
    first, rest = pl.ds(0, 128), pl.ds(128, both - 128)
    first_in = started(got_hbm.at[:, first], got_ref.at[:, first], sems.at[0])
    rest_in = started(got_hbm.at[:, rest], got_ref.at[:, rest], sems.at[1])
    wo_u_in = started(wo_u_hbm, wo_u_ref, sems.at[4])
    before = iota((slots, slots), 0) <= iota((slots, slots), 1)
    before_ref[...] = jnp.where(before, 1.0, 0.0).astype(BF)
    lane0 = jnp.where(iota((8, 128), 1) == 0, 1.0, 0.0).astype(BF)
    first_in.wait()
    live_row = dot_nt(lane0, got_ref[:, :128]) < EMPTY_MARK / 2
    place_row = dot(jnp.where(live_row, 1.0, 0.0).astype(BF), before_ref[...])
    place_row = jnp.where(live_row, place_row - 1.0, -1.0)[:1, :]
    narrow = jnp.where(iota((live_rows, slots), 0).astype(F32) == place_row, 1.0, 0.0).astype(BF)
    narrow_ref[...] = narrow
    narrow_out = started(narrow_ref, narrow_hbm, sems.at[2])
    widen_ref[...] = narrow_ref[...].T
    rest_in.wait()
    rows_ref[...] = dot(narrow, got_ref[...]).astype(BF)
    rows_out = started(rows_ref, rows_hbm, sems.at[3])
    mine = rows_ref[:, :width]
    other = rows_ref[:, width:]
    total_ref[:, :hidden] = dot(mine, wg_ref[...]) + dot(other, wo_g_ref[...])
    wo_u_in.wait()
    total_ref[:, hidden:] = dot(mine, wu_ref[...]) + dot(other, wo_u_ref[...])
    send_chunks(ids, total_ref, own_ref, (s1, s2, s3))
    narrow_out.wait()
    rows_out.wait()


def activate(ids, own_ref, r1, r2, r3, pre_ref, hidden_ref):
    hidden = hidden_ref.shape[1]
    pre = own_ref[...] + r1[...].astype(F32) + r2[...].astype(F32) + r3[...].astype(F32)
    pre_ref[...] = pre
    hidden_ref[...] = (jax.nn.silu(pre[:, :hidden]) * pre[:, hidden:]).astype(BF)


def forward_out(ids, h0, h1, h2, h3, wd_ref, wo_d_ref, widen_ref, pre_ref, hidden_hbm, sent_ref,
                widen_hbm, pre_hbm, buffer, sems, hidden_ref, more_sems):
    kept = [
        started(widen_ref, widen_hbm, more_sems.at[0]),
        started(pre_ref, pre_hbm, more_sems.at[1]),
    ]
    join_chunks(ids, (h0, h1, h2, h3), hidden_ref)
    kept.append(started(hidden_ref, hidden_hbm, more_sems.at[2]))
    half = wd_ref.shape[1] // 2
    leave_blocks(
        [
            lambda out=out, at=at: dot(widen_ref[...], out[:, at : at + half]).astype(BF)
            for out in (
                dot(hidden_ref[...], wd_ref[...]).astype(BF),
                dot(hidden_ref[...], wo_d_ref[...]).astype(BF),
            )
            for at in (0, half)
        ],
        buffer, sent_ref, sems,
    )
    for copy in kept:
        copy.wait()


def backward_in(ids, got_hbm, narrow_hbm, wd_hbm, wo_d_hbm, rows_hbm, own_ref, s1, s2, s3,
                total_ref, got_ref, narrow_ref, wd_ref, wo_d_ref, rows_ref, sems):
    width = wd_ref.shape[1]
    narrow_in = started(narrow_hbm, narrow_ref, sems.at[0])
    mine, other = pl.ds(0, width), pl.ds(width, width)
    mine_in = started(got_hbm.at[:, mine], got_ref.at[:, mine], sems.at[1])
    other_in = started(got_hbm.at[:, other], got_ref.at[:, other], sems.at[2])
    wd_in = started(wd_hbm, wd_ref, sems.at[3])
    wo_d_in = started(wo_d_hbm, wo_d_ref, sems.at[4])
    narrow_in.wait()
    mine_in.wait()
    rows_ref[:, :width] = dot(narrow_ref[...], got_ref[:, :width]).astype(BF)
    other_in.wait()
    rows_ref[:, width:] = dot(narrow_ref[...], got_ref[:, width:]).astype(BF)
    rows_out = started(rows_ref, rows_hbm, sems.at[5])
    wd_in.wait()
    total_ref[...] = dot_nt(rows_ref[:, :width], wd_ref[...])
    wo_d_in.wait()
    total_ref[...] += dot_nt(rows_ref[:, width:], wo_d_ref[...])
    send_chunks(ids, total_ref, own_ref, (s1, s2, s3))
    rows_out.wait()


def deactivate(ids, own_ref, r1, r2, r3, pre_ref, out_ref):
    hidden = own_ref.shape[1]
    grad = own_ref[...] + r1[...].astype(F32) + r2[...].astype(F32) + r3[...].astype(F32)
    gate_pre = pre_ref[:, :hidden]
    up_pre = pre_ref[:, hidden:]
    sigma = jax.nn.sigmoid(gate_pre)
    slope = sigma * (1.0 + gate_pre * (1.0 - sigma))
    out_ref[:, :hidden] = (grad * up_pre * slope).astype(BF)
    out_ref[:, hidden:] = (grad * (gate_pre * sigma)).astype(BF)


def backward_out(ids, g0, g1, g2, g3, wg_ref, wu_ref, wo_g_ref, wo_u_ref, widen_ref,
                 grads_hbm, sent_ref, buffer, sems, grads_ref, grads_sems):
    join_chunks(ids, (g0, g1, g2, g3), grads_ref)
    grads_out = started(grads_ref, grads_hbm, grads_sems.at[0])
    hidden = wg_ref.shape[1]
    gate = grads_ref[:, :hidden]
    up = grads_ref[:, hidden:]
    widen = widen_ref[...]

    def half(gate_w, up_w):
        back = dot_nt(gate, gate_w[...]) + dot_nt(up, up_w[...])
        return dot(widen, back.astype(BF)).astype(BF)

    leave_blocks(
        [lambda: half(wg_ref, wu_ref), lambda: half(wo_g_ref, wo_u_ref)], buffer, sent_ref, sems
    )
    grads_out.wait()


def fetch(ids, source_hbm, out_ref, sems):
    started(source_hbm, out_ref, sems.at[0]).wait()


def combine_out(ids, back_hbm, own_hbm, other_hbm, slot_ref, gate_ref, mine_hbm, theirs_ref,
                dots_ref, back_ref, own_ref, other_ref, mine_ref, sems):
    slots, both = back_ref.shape
    count, width = own_ref.shape
    pair = slot_ref.shape[0]
    mine, other = pl.ds(0, width), pl.ds(width, width)
    back_mine = started(back_hbm.at[:, mine], back_ref.at[:, mine], sems.at[0])
    own_in = started(own_hbm, own_ref, sems.at[1])
    back_other = started(back_hbm.at[:, other], back_ref.at[:, other], sems.at[2])
    other_in = started(other_hbm, other_ref, sems.at[3])
    token_row = slot_row(slot_ref[...].astype(F32), ids[0], slots)
    gate_row = slot_row(gate_ref[...].astype(F32), ids[0], slots)
    adder = jnp.where(
        iota((count, slots), 0).astype(F32) == token_row, gate_row, 0.0
    ).astype(BF)
    token, picker = row_picker(slot_ref, ids, slots, count)
    back_mine.wait()
    mine_ref[...] = dot(adder, back_ref[:, :width])
    mine_out = started(mine_ref, mine_hbm, sems.at[4])
    own_in.wait()
    sums = jnp.sum(
        dot(picker, own_ref[...]) * back_ref[:, :width].astype(F32), axis=1, keepdims=True
    )
    back_other.wait()
    theirs_ref[...] = dot(adder, back_ref[:, width:])
    other_in.wait()
    sums = sums + jnp.sum(
        dot(picker, other_ref[...]) * back_ref[:, width:].astype(F32), axis=1, keepdims=True
    )
    here = iota((slots, pair), 1) == iota((slots, pair), 0) % pair
    spread = jnp.where(here, sums, 0.0)
    dots_ref[...] = jnp.sum(spread.reshape(slots // pair, pair, pair), axis=1)
    mine_out.wait()


def place_dots(ids, mine_ref, other_ref, out_ref):
    owners, experts = mine_ref.shape[0], out_ref.shape[1]
    out = jnp.zeros(out_ref.shape, F32)
    for ref, core in ((mine_ref, ids[0]), (other_ref, 1 - ids[0])):
        expert = 2 * iota((owners, experts), 0) + core
        there = jnp.where(iota((owners, experts), 1) == expert, 1.0, 0.0).astype(BF)
        out = out + dot_tn(ref[...], there)
    out_ref[...] = out.astype(BF)


def adder_of(ids, slot_ref, count, slots):
    token_row = slot_row(slot_ref[...].astype(F32), ids[0], slots)
    return jnp.where(iota((count, slots), 0).astype(F32) == token_row, 1.0, 0.0).astype(BF)


def combine_theirs(ids, back_ref, slot_ref, theirs_ref):
    count, width = theirs_ref.shape
    adder = adder_of(ids, slot_ref, count, back_ref.shape[0])
    theirs_ref[...] = dot(adder, back_ref[:, width:])


def combine_mine(ids, back_ref, slot_ref, mine_ref):
    count, width = mine_ref.shape
    adder = adder_of(ids, slot_ref, count, back_ref.shape[0])
    mine_ref[...] = dot(adder, back_ref[:, :width])


def load_rows(rows_in_hbm, grads_hbm, hidden_hbm, rows_grad_hbm, at, refs, sems):
    sources = (rows_in_hbm.at[:, at], grads_hbm, rows_grad_hbm.at[:, at], hidden_hbm)
    return [started(source, ref, sems.at[n]) for n, (source, ref) in enumerate(zip(sources, refs))]


def weights_theirs(ids, rows_in_hbm, grads_hbm, hidden_hbm, rows_grad_hbm, in_ref, down_ref,
                   rows_in_ref, grads_ref, rows_grad_ref, hidden_ref, sems):
    width = in_ref.shape[0]
    loads = load_rows(rows_in_hbm, grads_hbm, hidden_hbm, rows_grad_hbm, pl.ds(width, width),
                      (rows_in_ref, grads_ref, rows_grad_ref, hidden_ref), sems)
    loads[0].wait()
    loads[1].wait()
    in_ref[...] = dot_tn(rows_in_ref[...], grads_ref[...]).astype(BF)
    loads[2].wait()
    loads[3].wait()
    down_ref[...] = dot_tn(hidden_ref[...], rows_grad_ref[...]).astype(BF)


def weights_mine(ids, rows_in_hbm, grads_hbm, hidden_hbm, rows_grad_hbm, gate_ref, up_ref, down_ref,
                 rows_in_ref, grads_ref, rows_grad_ref, hidden_ref, mine_in, mine_down, sems):
    width, hidden = gate_ref.shape[1:]
    core = ids[0]
    loads = load_rows(rows_in_hbm, grads_hbm, hidden_hbm, rows_grad_hbm, pl.ds(0, width),
                      (rows_in_ref, grads_ref, rows_grad_ref, hidden_ref), sems)
    loads[0].wait()
    loads[1].wait()
    mine_in[...] = dot_tn(rows_in_ref[...], grads_ref[...]).astype(BF)
    stores = [
        started(mine_in.at[:, pl.ds(0, hidden)], gate_ref.at[core], sems.at[4]),
        started(mine_in.at[:, pl.ds(hidden, hidden)], up_ref.at[core], sems.at[5]),
    ]
    loads[2].wait()
    loads[3].wait()
    mine_down[...] = dot_tn(hidden_ref[...], rows_grad_ref[...]).astype(BF)
    stores.append(started(mine_down, down_ref.at[core], sems.at[6]))
    for store in stores:
        store.wait()


def weights_got(ids, got_in_ref, got_down_ref, gate_in, up_in, down_in, gate_ref, up_ref, down_ref,
                sems):
    hidden = gate_ref.shape[2]
    there = 1 - ids[0]
    stores = [
        started(got_in_ref.at[:, pl.ds(0, hidden)], gate_ref.at[there], sems.at[0]),
        started(got_in_ref.at[:, pl.ds(hidden, hidden)], up_ref.at[there], sems.at[1]),
        started(got_down_ref, down_ref.at[there], sems.at[2]),
    ]
    for store in stores:
        store.wait()


def local(tokens, out_grad, slot_token, slot_gate, w_gate, w_up, w_down):
    senders = lax.axis_size("expert")
    devices = lax.axis_size("dp")
    parts = devices // 2
    count, width = tokens.shape
    both = 2 * width
    experts, pair = slot_token.shape[1:]
    hidden = w_gate.shape[2]
    slots = senders * pair
    chunk = LIVE // parts
    place = lax.axis_index("dp")
    core = place % 2
    ids = jnp.stack([core, place // 2]).astype(jnp.int32)
    slot_table = slot_token[0].T
    gate_table = slot_gate[0].T

    def swap(value):
        return lax.ppermute(value, "dp", [(i, i ^ 1) for i in range(devices)])

    def along(value, k):
        return lax.ppermute(value, "dp", [(i, (i + 2 * k) % devices) for i in range(devices)])

    def spread(values):
        return [along(value, k + 1) for k, value in enumerate(values)]

    def gather_x(value):
        return [value] + spread([value] * (parts - 1))

    def exchange(value):
        value = value.reshape(senders, pair, both)
        value = lax.all_to_all(value, "expert", split_axis=0, concat_axis=0, tiled=True)
        return value.reshape(slots, both)

    def pick_expert(value, which):
        return lax.dynamic_index_in_dim(value, which, 0, keepdims=False)

    tok_other = swap(tokens)
    grad_other = swap(out_grad)
    wg, wu, wd = (pick_expert(w, core) for w in (w_gate, w_up, w_down))
    wo_g, wo_u, wo_d = (swap(pick_expert(w, 1 - core)) for w in (w_gate, w_up, w_down))
    picks = 4 * slots * count * width
    move = 4 * LIVE * slots * width
    mm = 4 * LIVE * width * hidden
    sent = ((slots, both), BF)
    buffers = [pltpu.VMEM((slots, both), BF), pltpu.SemaphoreType.DMA((4,))]

    def room(*shapes):
        return [pltpu.VMEM(shape, dtype) for shape, dtype in shapes]

    def sems(n):
        return [pltpu.SemaphoreType.DMA((n,))]

    own_half, picker = call(
        pick_own, ids, (slot_table, tokens), [((slots, width), BF), ((slots, count), BF)],
        picks // 2, room((slot_table.shape, jnp.int32), (tokens.shape, BF)) + sems(2), (), (0, 1),
    )
    (sent_in,) = call(
        pick_other, ids, (own_half, picker, tok_other), [sent], picks // 2,
        room(((slots, width), BF)) + sems(3), (0,),
    )
    got_in = exchange(sent_in)
    (sent_grad,) = call(
        pick_grads, ids, (slot_table, gate_table, out_grad, grad_other), [sent], picks, buffers, (0,)
    )
    sent_grad, wg, wu, wd, wo_g, wo_u, wo_d = lax.optimization_barrier(
        (sent_grad, wg, wu, wd, wo_g, wo_u, wo_d)
    )
    got_grad = exchange(sent_grad)

    rows_in, narrow, widen, own, *sends = call(
        forward_in,
        ids,
        (got_in, wo_u, wg, wu, wo_g),
        [
            ((LIVE, both), BF),
            ((LIVE, slots), BF),
            ((slots, LIVE), BF),
            ((chunk, 2 * hidden), F32),
        ]
        + [((chunk, 2 * hidden), BF)] * (parts - 1),
        move + 2 * mm,
        room(
            ((LIVE, 2 * hidden), F32),
            ((slots, both), BF),
            ((LIVE, both), BF),
            ((LIVE, slots), BF),
            ((width, hidden), BF),
            ((slots, slots), BF),
        )
        + sems(5),
        (0, 1),
        (0, 1),
    )
    pre, hidden_own = call(
        activate,
        ids,
        (own, *spread(sends)),
        [((chunk, 2 * hidden), F32), ((chunk, hidden), BF)],
        8 * chunk * hidden,
    )
    hidden_all, sent_out, widen, pre = call(
        forward_out,
        ids,
        (*gather_x(hidden_own), wd, wo_d, widen, pre),
        [((LIVE, hidden), BF), sent, ((slots, LIVE), BF), ((chunk, 2 * hidden), F32)],
        move + mm,
        buffers + room(((LIVE, hidden), BF)) + sems(3),
        (0, 1, 2, 3),
    )
    back_out = exchange(sent_out)

    rows_grad, own, *sends = call(
        backward_in,
        ids,
        (got_grad, narrow, wd, wo_d),
        [((LIVE, both), BF), ((chunk, hidden), F32)] + [((chunk, hidden), BF)] * (parts - 1),
        move + mm,
        room(
            ((LIVE, hidden), F32),
            ((slots, both), BF),
            ((LIVE, slots), BF),
            ((hidden, width), BF),
            ((hidden, width), BF),
            ((LIVE, both), BF),
        )
        + sems(6),
        (0,),
        (0, 1, 2, 3),
    )
    (pre_grads,) = call(
        deactivate,
        ids,
        (own, *spread(sends), pre),
        [((chunk, 2 * hidden), BF)],
        12 * chunk * hidden,
    )
    wo_u, pre_grads = lax.optimization_barrier((wo_u, pre_grads))
    (wo_u,) = call(fetch, ids, (wo_u,), [(wo_u.shape, BF)], 0, sems(1), (), (0,))
    grads_all, sent_back = call(
        backward_out,
        ids,
        (*gather_x(pre_grads), wg, wu, wo_g, wo_u, widen),
        [((LIVE, 2 * hidden), BF), sent],
        move + 2 * mm,
        buffers + room(((LIVE, 2 * hidden), BF)) + sems(1),
        (0, 1),
    )
    back_grad = exchange(sent_back)

    out_mine, out_theirs, dots = call(
        combine_out,
        ids,
        (back_out, out_grad, grad_other, slot_table, gate_table),
        [((count, width), F32), ((count, width), F32), ((senders, pair), F32)],
        2 * picks,
        room(
            ((slots, both), BF), ((count, width), BF), ((count, width), BF), ((count, width), F32)
        )
        + sems(5),
        (0,),
        (0, 1, 2),
    )
    rows_in, grads_all, hidden_all, rows_grad, out_theirs, dots = lax.optimization_barrier(
        (rows_in, grads_all, hidden_all, rows_grad, out_theirs, dots)
    )
    rows = (rows_in, grads_all, hidden_all, rows_grad)
    rows_room = room(
        ((LIVE, width), BF), ((LIVE, 2 * hidden), BF), ((LIVE, width), BF), ((LIVE, hidden), BF)
    )
    theirs_in, theirs_down = call(
        weights_theirs,
        ids,
        rows,
        [((width, 2 * hidden), BF), ((hidden, width), BF)],
        3 * mm // 2,
        rows_room + sems(4),
        (),
        (0, 1, 2, 3),
    )
    weight_shapes = [(w_gate.shape, BF), (w_up.shape, BF), (w_down.shape, BF)]
    weight_grads = call(
        weights_mine,
        ids,
        rows,
        weight_shapes,
        3 * mm // 2,
        rows_room + room(((width, 2 * hidden), BF), ((hidden, width), BF)) + sems(7),
        (0, 1, 2),
        (0, 1, 2, 3),
    )
    moe_out = (out_mine + swap(out_theirs)).astype(BF)
    *dots, weight_grads = lax.optimization_barrier((*gather_x(dots), weight_grads))
    dots = sum(dots).astype(BF)
    (gate_grad,) = call(
        place_dots, ids, (dots, swap(dots)), [((pair, experts), BF)], 4 * pair * experts * senders
    )
    grad_gate_w, grad_up_w, grad_down_w = call(
        weights_got,
        ids,
        (swap(theirs_in), swap(theirs_down), *weight_grads),
        weight_shapes,
        0,
        sems(3),
        (0, 1, 2),
        (2, 3, 4),
        ((2, 0), (3, 1), (4, 2)),
    )
    back_grad, moe_out, gate_grad, grad_gate_w, grad_up_w, grad_down_w = lax.optimization_barrier(
        (back_grad, moe_out, gate_grad, grad_gate_w, grad_up_w, grad_down_w)
    )
    half = [((count, width), F32)]
    (tok_theirs,) = call(combine_theirs, ids, (back_grad, slot_table), half, picks // 2)
    (tok_mine,) = call(combine_mine, ids, (back_grad, slot_table), half, picks // 2)
    token_grad = (tok_mine + swap(tok_theirs)).astype(BF)
    gate_grad = gate_grad.T.reshape(1, experts, pair)
    return (moe_out, token_grad, gate_grad, grad_gate_w, grad_up_w, grad_down_w)


def solution(mesh):
    placed = (
        P("expert", "dp"),
        P("expert", "dp"),
        P("expert", None, None),
        P("expert", None, None),
        P("expert", "dp", None),
        P("expert", "dp", None),
        P("expert", None, "dp"),
    )
    return jax.shard_map(
        local,
        mesh=mesh,
        in_specs=placed,
        out_specs=(
            P("expert", "dp"),
            P("expert", "dp"),
            P("expert", None, None),
            P("expert", "dp", None),
            P("expert", "dp", None),
            P("expert", None, "dp"),
        ),
        check_vma=False,
    )
```
